256 devices in a mesh: grp: 8 (over y, core), path: 32 (over x, z).
Axes of the slice: x: 4, y: 4, z: 8, core: 2. Of those that a mesh axis runs over, the one named last changes fastest.
Arguments:
- start_rates: float32 [256, 80], P('grp'), may hold values from 1 to 6
- loadings: float32 [256, 80, 80], P('grp'), may hold values from -0.15625 to 0.15625
- stress: float32 [80], replicated, may hold values from 0.5 to 1.5
- increments: bfloat16 [256, 2, 80, 8192], P('grp', None, None, 'path'), may hold values from -6 to 6
- cotangent: float32 [256, 80, 8192], P('grp', None, 'path'), may hold values from 0.5 to 1.5
- first_active: int32 [256], P('grp'), may hold values from 0 to 39
Outputs:
- rate_adjoint: float32 [256, 80], P(('grp', 'path'))
- vol_gradient: float32 [256, 80, 80], P(('grp', 'path'))
- stress_gradient: float32 [80], replicated
The draws below stay inside these ranges and needn't reach their ends.
Inputs may be any that keep to these rules, and one draw needn't show every extreme that they name: `first_active`: rates below a scenario's first active index have expired and stay fixed.
All inputs are finite; a program needn't handle non-finite values.
Results may differ from the reference program's by a relative error of at most 0.0003.
Values sent between devices are 32-bit elements; how exact they have to be, the bound alone decides.
A program may use at most 64 MiB of HBM per device.

```python
import jax
import jax.numpy as jnp
from jax import lax

NR = 80
F = 80
SCEN = 256
PATHS = 8192


def plant(result, stream_key, smallest, largest):
    place = [jax.random.randint(jax.random.fold_in(stream_key, axis), (), 0, length) for axis, length in enumerate(result.shape)]
    main_axis = result.shape.index(max(result.shape))
    beside = place[:main_axis] + [(place[main_axis] + 1) % result.shape[main_axis]] + place[main_axis + 1:]
    return result.at[tuple(place)].set(smallest).at[tuple(beside)].set(largest)


def block_levels(own_key, extent, pieces, least, top_value):
    def one(position, shards_of):
        heights = jax.random.uniform(jax.random.fold_in(jax.random.fold_in(own_key, 6), position), (shards_of,), jnp.float32, least / len(pieces), top_value / len(pieces))
        return jnp.repeat(jnp.exp(heights), extent[position] // shards_of).reshape((-1,) + (1,) * (len(extent) - position - 1))

    gain = one(*pieces[0])
    for cut in pieces[1:]:
        gain = gain * one(*cut)
    return gain


def normal_values(own_key, extent, scale, bound, split=(), kind=jnp.bfloat16):
    entries = scale * jax.random.normal(own_key, extent, jnp.float32)
    if split:
        entries = entries * block_levels(own_key, extent, split, -0.22, 0.18)
    return jnp.clip(entries, -bound, bound).astype(kind)


def setup_inputs(seed: int = 0) -> dict:
    arg_keys = jax.random.split(jax.random.key(seed), 7)
    return {
        "start_rates": jnp.clip(1.0 + 5.0 * jax.random.uniform(arg_keys[0], (SCEN, NR), jnp.float32) ** block_levels(arg_keys[0], (SCEN, NR), ((0, 8),), -0.2, 0.2), 1.0, 6.0),
        "loadings": normal_values(arg_keys[1], (SCEN, NR, F), (16 * F) ** -0.5, 0.15625, ((0, 8),), jnp.float32),
        "stress": jnp.clip(1.0 + 0.1 * jax.random.normal(arg_keys[2], (NR,), jnp.float32), 0.5, 1.5),
        "increments": normal_values(arg_keys[3], (SCEN, 2, F, PATHS), 1.0, 6.0, ((0, 8), (3, 32))),
        "cotangent": jnp.clip(0.5 + 1.0 * jax.random.uniform(arg_keys[4], (SCEN, NR, PATHS), jnp.float32) ** block_levels(arg_keys[4], (SCEN, NR, PATHS), ((0, 8), (2, 32)), -0.2, 0.2), 0.5, 1.5),
        "first_active": plant(jax.random.randint(arg_keys[5], (SCEN,), 0, NR // 2), jax.random.fold_in(arg_keys[5], 1), 0, (NR // 2) - 1).astype(jnp.int32),
    }


RATE_SCALE = 0.01

def advance(rates, lam, active, shocks):
    highest = lax.Precision.HIGHEST
    cov = jnp.einsum('sif,sjf->sij', lam, lam, precision=highest)
    count = lam.shape[1]
    lower = (jnp.arange(count)[:, None] >= jnp.arange(count)[None, :]).astype(jnp.float32)
    accrual = active * (RATE_SCALE * rates / (1.0 + RATE_SCALE * rates))
    drift = jnp.einsum('sij,sjp->sip', cov * lower[None], accrual, precision=highest)
    half_var = 0.5 * jnp.diagonal(cov, axis1=1, axis2=2)[:, :, None]
    shock = jnp.einsum('sif,sfp->sip', lam, shocks, precision=highest)
    return rates * jnp.exp(active * (drift - half_var + shock))

def reference(start_rates, loadings, stress, increments, cotangent, first_active):
    rate_index = jnp.arange(loadings.shape[1]).astype(jnp.int32)

    def one_scenario(inputs):
        start, load, incr, cot, first = inputs
        active = (rate_index >= first).astype(jnp.float32)[None, :, None]
        lam = (stress[:, None] * load)[None]
        early = incr[0].astype(jnp.float32)[None]
        late = incr[1].astype(jnp.float32)[None]
        width = cot.shape[1]

        def first_step(rates0, lam_in):
            spread = jnp.broadcast_to(rates0[:, :, None], (1, rates0.shape[1], width))
            return advance(spread, lam_in, active, early)

        def second_step(rates1, lam_in):
            return advance(rates1, lam_in, active, late)
        mid, back_first = jax.vjp(first_step, start[None], lam)
        final, back_second = jax.vjp(second_step, mid, lam)
        bar_mid, bar_late = back_second((cot / PATHS)[None])
        bar_start, bar_early = back_first(bar_mid)
        return (bar_start[0], bar_early[0] + bar_late[0])
    rate_adjoint, bar_lam = lax.map(one_scenario, (start_rates, loadings, increments, cotangent, first_active))
    vol_gradient = stress[None, :, None] * bar_lam
    stress_gradient = lax.optimization_barrier(jnp.sum(loadings * bar_lam, axis=(0, 2)))
    return (rate_adjoint, vol_gradient, stress_gradient)
```

```python
import math

import jax
import jax.numpy as jnp
from jax import lax
from jax.experimental import pallas as pl
from jax.experimental.pallas import tpu as pltpu
from jax.sharding import PartitionSpec as P

NR = 80
WIDTH = 256
X, Z, G = 4, 8, 8
PAIRS = 16
PACKED = 56
LN2 = math.log(2.0)
LOG2E = 1.0 / LN2
bf16 = jnp.bfloat16
f32 = jnp.float32
MESH = pl.DeviceIdType.MESH


def dot(a, b):
    return jnp.dot(a, b, preferred_element_type=f32)


def dot_nt(a, b):
    return lax.dot_general(a, b, (((1,), (1,)), ((), ())), preferred_element_type=f32)


def split(value):
    high = value.astype(bf16)
    return high, (value - high.astype(f32)).astype(bf16)


def index_masks():
    rows = lax.broadcasted_iota(jnp.int32, (NR, NR), 0)
    cols = lax.broadcasted_iota(jnp.int32, (NR, NR), 1)
    return rows, cols


def pair_place(pair, z):
    step, way = pair // 2, pair % 2
    reach = 4 - (step + 1) // 2
    target = lax.rem(z + reach * (1 - way) + (Z - reach) * way, Z)
    return target, lax.rem(step + way, 2)


def scaled_loadings(load, stress_col, first, rows):
    return jnp.where(rows >= first, load * stress_col, 0.0) * LOG2E


def adjoint_of(items, stress_col, log_paths, emit):
    rows, cols = index_masks()
    low, upp, eye = rows >= cols, rows <= cols, rows == cols
    ones = jnp.ones((16, WIDTH), bf16)
    gap = jnp.zeros((32, WIDTH), bf16)
    for d in items:
        d["lam"] = scaled_loadings(d["load"][...], stress_col, d["first"], rows)
        d["lh"], d["ll"] = split(d["lam"])
    for d in items:
        d["cov"] = dot_nt(d["lh"], d["lh"])
    for d in items:
        drift = jnp.where(low, d["cov"], 0.0) * LN2
        r0 = d["r0"]
        d["a0"] = r0 / (100.0 + r0)
        half = jnp.sum(d["lam"] * d["lam"], axis=1, keepdims=True) * (-0.5 * LN2)
        d["c1"] = half + jnp.sum(drift * d["a0"] + jnp.where(eye, jnp.log2(r0), 0.0), axis=1, keepdims=True)
        d["c2"] = half - log_paths
        d["left"] = jnp.concatenate([d["lh"], d["ll"], drift.astype(bf16)], axis=1)
        d["back"] = (jnp.where(upp, d["cov"], 0.0) * (LN2 * LN2)).astype(bf16)
    for d in items:
        z1 = d["z"][0]
        d["e1"] = dot(d["left"][:, : 2 * NR], jnp.concatenate([z1, z1], axis=0))
    for d in items:
        mid = jnp.exp2(d["e1"] + d["c1"])
        scaled = 0.01 * mid
        inverse = 1.0 / (1.0 + scaled)
        accrual = scaled * inverse
        d["mid"], d["a"], d["slope"] = mid, accrual.astype(bf16), accrual * inverse
    for d in items:
        z2 = d["z"][1]
        d["e2"] = dot(d["left"], jnp.concatenate([z2, z2, d["a"]], axis=0))
    for d in items:
        d["g2"] = d["mid"] * jnp.exp2(d["e2"] + d["c2"]) * d["cot"][...]
        d["g2h"], d["g2l"] = split(d["g2"])
    for d in items:
        d["da"] = dot(d["back"], d["g2h"])
    for d in items:
        right = jnp.concatenate([d["z"][1], ones, gap, d["a"]], axis=0)
        d["sums2"] = dot_nt(jnp.concatenate([d["g2h"], d["g2l"]], axis=0), right)
    for d in items:
        g1h, g1l = split(d["g2"] + d["slope"] * d["da"])
        right = jnp.concatenate([d["z"][0], ones], axis=0)
        d["sums1"] = dot_nt(jnp.concatenate([g1h, g1l], axis=0), right)
    for d in items:
        sum1 = d["sums1"][:NR] + d["sums1"][NR:]
        sum2 = d["sums2"][:NR, :128] + d["sums2"][NR:, :128]
        outer = d["sums2"][:NR, 128:208] + d["sums2"][NR:, 128:208]
        total1, total2 = sum1[:, NR : NR + 1], sum2[:, NR : NR + 1]
        bar_cov = jnp.where(low, outer + total1 * d["a0"], 0.0)
        mh, ml = split((bar_cov + bar_cov.T) * LN2)
        through = dot(
            jnp.concatenate([mh, ml, mh], axis=1), jnp.concatenate([d["lh"], d["lh"], d["ll"]], axis=0)
        )
        bar = sum1[:, :NR] + sum2[:, :NR] + through - ((total1 + total2) * LN2) * d["lam"]
        emit(d, jnp.where(rows >= d["first"], bar, 0.0), total1)


def pack(ref, bar, total):
    ref[:, 0:NR] = bar[:PACKED]
    ref[:, NR : NR + 1] = total[:PACKED]
    rest = jnp.concatenate([bar[PACKED:], total[PACKED:]], axis=1)
    ref[0:24, 81:128] = rest[:, 0:47]
    ref[24:48, 81:115] = rest[:, 47:81]
    ref[24:48, 115:128] = jnp.zeros((24, 13), f32)
    ref[48:56, 81:128] = jnp.zeros((8, 47), f32)


def unpack(value):
    rest = jnp.concatenate([value[0:24, 81:128], value[24:48, 81:115]], axis=1)
    bar = jnp.concatenate([value[:, 0:NR], rest[:, 0:NR]], axis=0)
    total = jnp.concatenate([value[:, NR : NR + 1], rest[:, NR : NR + 1]], axis=0)
    return bar, total


def kernel(
    log_paths,
    stress_ref, first_ref, start_ref, load_hbm, z_hbm, cot_hbm,
    rate_out, vol_out, stress_out,
    load_v, z_v, cot_v, out_buf, ring_buf, x_buf, acc, sx, sz, sg,
    in_sem, ring_send, ring_recv, x_send, x_recv, s_send, s_recv,
):
    g = lax.axis_index("grp")
    path = lax.axis_index("path")
    x, z = path // Z, lax.rem(path, Z)

    def fetches(pair):
        target, half = pair_place(pair, z)
        blocks = pl.ds(2 * half, 2)
        return [
            pltpu.make_async_copy(hbm.at[blocks, target], vmem.at[pair], in_sem.at[i, pair])
            for i, (hbm, vmem) in enumerate(((load_hbm, load_v), (z_hbm, z_v), (cot_hbm, cot_v)))
        ]

    @pl.loop(0, PAIRS)
    def _(pair):
        for copy in fetches(pair):
            copy.start()

    def x_peer(k):
        return (g, lax.rem(x + k, X) * Z + z)

    def z_peer(k):
        return (g, x * Z + lax.rem(z + k, Z))

    def g_peer(k):
        return (lax.rem(g + k, G), path)

    barrier = pltpu.get_barrier_semaphore()
    peers = [(x_peer, X), (z_peer, Z), (g_peer, G)]
    for peer, size in peers:
        for k in range(1, size):
            pl.semaphore_signal(barrier, inc=1, device_id=peer(k), device_id_type=MESH)

    rows, cols = index_masks()
    eye = rows == cols
    stress_col = jnp.sum(jnp.where(eye, stress_ref[...], 0.0), axis=1, keepdims=True)
    acc[...] = jnp.zeros_like(acc)

    def ring(way, step):
        return pltpu.make_async_remote_copy(
            src_ref=out_buf.at[2 * step + way],
            dst_ref=ring_buf.at[way, step],
            send_sem=ring_send.at[way, step],
            recv_sem=ring_recv.at[way, step],
            device_id=z_peer(Z - 1 if way else 1),
            device_id_type=MESH,
        )

    def emit(d, bar, total):
        pack(d["out"], bar, total)
        acc[...] += d["load"][...] * bar

    def scenario(pair, k):
        target, half = pair_place(pair, z)
        s = (2 * half + k) * Z + target
        return dict(
            load=load_v.at[pair, k], z=z_v.at[pair, k], cot=cot_v.at[pair, k], out=out_buf.at[pair, k],
            first=first_ref[s], r0=start_ref[pl.ds(s, 1), :],
        )

    @pl.loop(0, 4)
    def _(group):
        for j in range(4):
            for copy in fetches(4 * group + j):
                copy.wait()
        items = [scenario(4 * group + j, k) for j in range(4) for k in range(2)]
        adjoint_of(items, stress_col, log_paths, emit)

        @pl.when(group == 0)
        def _():
            pl.semaphore_wait(barrier, X + Z + G - 3)

        for j in range(2):
            step = 2 * group + j
            for way in range(2):

                @pl.when(group > 0)
                def _():
                    ring(way, step - 2).wait_recv()
                    out_buf[2 * step + way] += ring_buf[way, step - 2]

                @pl.when(step < 7)
                def _():
                    ring(way, step).start()

    def share(stage, buf, peer, size, me, base):
        return [
            pltpu.make_async_remote_copy(
                src_ref=buf.at[me],
                dst_ref=buf.at[me],
                send_sem=s_send.at[base + k],
                recv_sem=s_recv.at[base + k],
                device_id=peer(k),
                device_id_type=MESH,
            )
            for k in range(1, size)
        ]

    def summed(buf, size):
        total = buf[0]
        for i in range(1, size):
            total = total + buf[i]
        return total

    stress_part = jnp.sum(jnp.where(eye, jnp.sum(acc[...], axis=1, keepdims=True), 0.0), axis=0, keepdims=True)
    sx[x, :, 0:NR] = jnp.broadcast_to(stress_part, (8, NR))
    sx[x, :, NR:128] = jnp.zeros((8, 128 - NR), f32)
    stage_x = share(0, sx, x_peer, X, x, 0)
    for copy in stage_x:
        copy.start()

    for copy in stage_x:
        copy.wait_recv()
    sz[z] = summed(sx, X)
    stage_z = share(1, sz, z_peer, Z, z, X)
    for copy in stage_z:
        copy.start()

    for way in range(2):
        ring(way, 6).wait_recv()
        out_buf[15 - way] += ring_buf[way, 6]

    def mine(at):
        return out_buf.at[15 - at // 2, lax.rem(at, 2)]

    stage_out = [
        pltpu.make_async_remote_copy(
            src_ref=mine(lax.rem(x + k, X)),
            dst_ref=x_buf.at[k - 1],
            send_sem=x_send.at[k - 1],
            recv_sem=x_recv.at[k - 1],
            device_id=x_peer(k),
            device_id_type=MESH,
        )
        for k in range(1, X)
    ]
    for copy in stage_out:
        copy.start()

    for copy in stage_z:
        copy.wait_recv()
    sg[g] = summed(sz, Z)
    stage_g = share(2, sg, g_peer, G, g, X + Z)
    for copy in stage_g:
        copy.start()

    lam = scaled_loadings(load_v[15 - x // 2, lax.rem(x, 2)], stress_col, first_ref[path], rows)
    lh, ll = split(lam)
    cov = (dot_nt(lh, lh) + dot_nt(lh, ll) + dot_nt(ll, lh)) * (LN2 * LN2)
    r0 = start_ref[pl.ds(path, 1), :]

    for copy in stage_out:
        copy.wait_recv()
    bar, total = unpack(mine(x)[...] + x_buf[0] + x_buf[1] + x_buf[2])
    vol_out[0] = stress_col * bar
    through = jnp.sum(jnp.where(rows >= cols, cov, 0.0) * total, axis=0, keepdims=True)
    direct = jnp.sum(jnp.where(eye, total, 0.0), axis=0, keepdims=True)
    rate_out[...] = direct / r0 + through * (100.0 / ((100.0 + r0) * (100.0 + r0)))

    for copy in stage_g:
        copy.wait_recv()
    stress_out[...] = summed(sg, G)[0:1, 0:NR]

    @pl.loop(0, 7)
    def _(step):
        for way in range(2):
            ring(way, step).wait_send()

    for copy in stage_x + stage_z + stage_g + stage_out:
        copy.wait_send()


def body(start_rates, loadings, stress, increments, cotangent, first_active):
    log_paths = math.log2(WIDTH * X * Z)
    vmem = pl.BlockSpec(memory_space=pltpu.VMEM)
    smem = pl.BlockSpec(memory_space=pltpu.SMEM)
    anywhere = pl.BlockSpec(memory_space=pl.ANY)
    dma = pltpu.SemaphoreType.DMA
    rate, vol, stress_gradient = pl.pallas_call(
        lambda *refs: kernel(log_paths, *refs),
        out_shape=(
            jax.ShapeDtypeStruct((1, NR), f32),
            jax.ShapeDtypeStruct((1, NR, NR), f32),
            jax.ShapeDtypeStruct((1, NR), f32),
        ),
        in_specs=[vmem, smem, vmem, anywhere, anywhere, anywhere],
        out_specs=(vmem, vmem, vmem),
        scratch_shapes=[
            pltpu.VMEM((PAIRS, 2, NR, NR), f32),
            pltpu.VMEM((PAIRS, 2, 2, NR, WIDTH), bf16),
            pltpu.VMEM((PAIRS, 2, NR, WIDTH), f32),
            pltpu.VMEM((PAIRS, 2, PACKED, 128), f32),
            pltpu.VMEM((2, 7, 2, PACKED, 128), f32),
            pltpu.VMEM((X - 1, PACKED, 128), f32),
            pltpu.VMEM((NR, NR), f32),
            pltpu.VMEM((X, 8, 128), f32),
            pltpu.VMEM((Z, 8, 128), f32),
            pltpu.VMEM((G, 8, 128), f32),
            dma((3, PAIRS)),
            dma((2, 7)),
            dma((2, 7)),
            dma((X - 1,)),
            dma((X - 1,)),
            dma((X + Z + G,)),
            dma((X + Z + G,)),
        ],
        compiler_params=pltpu.CompilerParams(
            collective_id=0, has_side_effects=True, vmem_limit_bytes=56 * 2**20
        ),
        name="adjoint",
    )(
        stress[None],
        first_active,
        start_rates,
        loadings.reshape(X, Z, NR, NR),
        increments.reshape(X, Z, 2, NR, WIDTH),
        cotangent.reshape(X, Z, NR, WIDTH),
    )
    return rate, vol, stress_gradient[0]


def solution(mesh):
    return jax.shard_map(
        body,
        mesh=mesh,
        in_specs=(
            P("grp", None),
            P("grp", None, None),
            P(),
            P("grp", None, None, "path"),
            P("grp", None, "path"),
            P("grp"),
        ),
        out_specs=(P(("grp", "path"), None), P(("grp", "path"), None, None), P()),
        check_vma=False,
    )
```

```python
import math

import jax
import jax.numpy as jnp
from jax import lax
from jax.experimental import pallas as pl
from jax.experimental.pallas import tpu as pltpu
from jax.sharding import PartitionSpec as P

NR = 80
WIDTH = 256
X, Z = 4, 8
Y, CORES = 4, 2
SIXTEEN = X * Y
PAIRS = 16
PACKED = 56
LN2 = math.log(2.0)
LOG2E = 1.0 / LN2
bf16 = jnp.bfloat16
f32 = jnp.float32
MESH = pl.DeviceIdType.MESH


def dot(a, b):
    return jnp.dot(a, b, preferred_element_type=f32)


def dot_nt(a, b):
    return lax.dot_general(a, b, (((1,), (1,)), ((), ())), preferred_element_type=f32)


def split(value):
    high = value.astype(bf16)
    return high, (value - high.astype(f32)).astype(bf16)


def index_masks():
    rows = lax.broadcasted_iota(jnp.int32, (NR, NR), 0)
    cols = lax.broadcasted_iota(jnp.int32, (NR, NR), 1)
    return rows, cols


def place(pair, k, x, z):
    half, step, way = pair // 8, pair % 8 // 2, pair % 2
    reach = 2 - (step + 1) // 2
    side = lax.rem(step + way, 2)
    hops = 3 - 2 * half - side if k else 4 + 2 * half + side
    return lax.rem(x + reach * (1 - way) + (X - reach) * way, X), hops


def scaled_loadings(load, stress_col, first, rows):
    return jnp.where(rows >= first, load * stress_col, 0.0) * LOG2E


def adjoint_of(items, stress_col, log_paths, emit):
    rows, cols = index_masks()
    low, upp, eye = rows >= cols, rows <= cols, rows == cols
    ones = jnp.ones((16, WIDTH), bf16)
    gap = jnp.zeros((32, WIDTH), bf16)
    for d in items:
        d["lam"] = scaled_loadings(d["load"][...], stress_col, d["first"], rows)
        d["lh"], d["ll"] = split(d["lam"])
    for d in items:
        d["cov"] = dot_nt(d["lh"], d["lh"])
    for d in items:
        drift = jnp.where(low, d["cov"], 0.0) * LN2
        r0 = d["r0"]
        d["a0"] = r0 / (100.0 + r0)
        half = jnp.sum(d["lam"] * d["lam"], axis=1, keepdims=True) * (-0.5 * LN2)
        d["c1"] = half + jnp.sum(drift * d["a0"] + jnp.where(eye, jnp.log2(r0), 0.0), axis=1, keepdims=True)
        d["c2"] = half - log_paths
        d["left"] = jnp.concatenate([d["lh"], d["ll"], drift.astype(bf16)], axis=1)
        d["back"] = (jnp.where(upp, d["cov"], 0.0) * (LN2 * LN2)).astype(bf16)
    for d in items:
        z1 = d["z"][0]
        d["e1"] = dot(d["left"][:, : 2 * NR], jnp.concatenate([z1, z1], axis=0))
    for d in items:
        mid = jnp.exp2(d["e1"] + d["c1"])
        scaled = 0.01 * mid
        inverse = 1.0 / (1.0 + scaled)
        accrual = scaled * inverse
        d["mid"], d["a"], d["slope"] = mid, accrual.astype(bf16), accrual * inverse
    for d in items:
        z2 = d["z"][1]
        d["e2"] = dot(d["left"], jnp.concatenate([z2, z2, d["a"]], axis=0))
    for d in items:
        d["g2"] = d["mid"] * jnp.exp2(d["e2"] + d["c2"]) * d["cot"][...]
        d["g2h"], d["g2l"] = split(d["g2"])
    for d in items:
        d["da"] = dot(d["back"], d["g2h"])
    for d in items:
        right = jnp.concatenate([d["z"][1], ones, gap, d["a"]], axis=0)
        d["sums2"] = dot_nt(jnp.concatenate([d["g2h"], d["g2l"]], axis=0), right)
    for d in items:
        g1h, g1l = split(d["g2"] + d["slope"] * d["da"])
        right = jnp.concatenate([d["z"][0], ones], axis=0)
        d["sums1"] = dot_nt(jnp.concatenate([g1h, g1l], axis=0), right)
    for d in items:
        sum1 = d["sums1"][:NR] + d["sums1"][NR:]
        sum2 = d["sums2"][:NR, :128] + d["sums2"][NR:, :128]
        outer = d["sums2"][:NR, 128:208] + d["sums2"][NR:, 128:208]
        total1, total2 = sum1[:, NR : NR + 1], sum2[:, NR : NR + 1]
        bar_cov = jnp.where(low, outer + total1 * d["a0"], 0.0)
        mh, ml = split((bar_cov + bar_cov.T) * LN2)
        through = dot(
            jnp.concatenate([mh, ml, mh], axis=1), jnp.concatenate([d["lh"], d["lh"], d["ll"]], axis=0)
        )
        bar = sum1[:, :NR] + sum2[:, :NR] + through - ((total1 + total2) * LN2) * d["lam"]
        emit(d, jnp.where(rows >= d["first"], bar, 0.0), total1)


def pack(ref, bar, total):
    ref[:, 0:NR] = bar[:PACKED]
    ref[:, NR : NR + 1] = total[:PACKED]
    rest = jnp.concatenate([bar[PACKED:], total[PACKED:]], axis=1)
    ref[0:24, 81:128] = rest[:, 0:47]
    ref[24:48, 81:115] = rest[:, 47:81]
    ref[24:48, 115:128] = jnp.zeros((24, 13), f32)
    ref[48:56, 81:128] = jnp.zeros((8, 47), f32)


def unpack(value):
    rest = jnp.concatenate([value[0:24, 81:128], value[24:48, 81:115]], axis=1)
    bar = jnp.concatenate([value[:, 0:NR], rest[:, 0:NR]], axis=0)
    total = jnp.concatenate([value[:, NR : NR + 1], rest[:, NR : NR + 1]], axis=0)
    return bar, total


def kernel(
    log_paths,
    stress_hbm, first_hbm, start_hbm, load_hbm, z_hbm, cot_hbm,
    out_hbm,
    stress_ref, first_ref, start_ref, out,
    load_v, z_v, cot_v, out_buf, ring_buf, z_buf, acc, s_plane, s_line,
    small_sem, out_sem, in_sem, ring_send, ring_recv, z_send, z_recv, s_send, s_recv,
):
    g = lax.axis_index("grp")
    path = lax.axis_index("path")
    x, z = path // Z, lax.rem(path, Z)

    def owner(pair, k):
        owner_x, hops = place(pair, k, x, z)
        return owner_x, lax.rem(z + hops, Z)

    def fetches(pair):
        return [
            pltpu.make_async_copy(hbm.at[owner(pair, k)], vmem.at[pair, k], in_sem.at[i, pair, k])
            for k in range(2)
            for i, (hbm, vmem) in enumerate(((load_hbm, load_v), (z_hbm, z_v), (cot_hbm, cot_v)))
        ]

    small = [
        pltpu.make_async_copy(hbm, here, small_sem.at[i])
        for i, (hbm, here) in enumerate(((stress_hbm, stress_ref), (first_hbm, first_ref), (start_hbm, start_ref)))
    ]
    for copy in small:
        copy.start()

    @pl.loop(0, PAIRS)
    def _(pair):
        for copy in fetches(pair):
            copy.start()

    def x_peer(k):
        return (g, lax.rem(x + k, X) * Z + z)

    def z_peer(k):
        return (g, x * Z + lax.rem(z + k, Z))

    y, core = g // CORES, lax.rem(g, CORES)

    def plane_peer(k):
        return (lax.rem(y + k // X, Y) * CORES + core, lax.rem(x + k % X, X) * Z + z)

    def line_peer(k):
        return (y * CORES + lax.rem(core + k // Z, CORES), x * Z + lax.rem(z + k % Z, Z))

    barrier = pltpu.get_barrier_semaphore()
    for k in range(1, SIXTEEN):
        for peer in (plane_peer, line_peer):
            pl.semaphore_signal(barrier, inc=1, device_id=peer(k), device_id_type=MESH)

    for copy in small:
        copy.wait()
    rows, cols = index_masks()
    eye = rows == cols
    stress_col = jnp.sum(jnp.where(eye, stress_ref[...], 0.0), axis=1, keepdims=True)
    acc[...] = jnp.zeros_like(acc)

    def ring(way, half, step):
        return pltpu.make_async_remote_copy(
            src_ref=out_buf.at[8 * half + 2 * step + way],
            dst_ref=ring_buf.at[way, half, step],
            send_sem=ring_send.at[way, half, step],
            recv_sem=ring_recv.at[way, half, step],
            device_id=x_peer(X - 1 if way else 1),
            device_id_type=MESH,
        )

    def hand_over(half, side, k):
        hops = 3 - 2 * half - side if k else 4 + 2 * half + side
        return pltpu.make_async_remote_copy(
            src_ref=out_buf.at[8 * half + 7 - side, k],
            dst_ref=z_buf.at[hops - 1],
            send_sem=z_send.at[hops - 1],
            recv_sem=z_recv.at[hops - 1],
            device_id=z_peer(hops),
            device_id_type=MESH,
        )

    handed = [(0, side, k) for side in range(2) for k in range(2)], [(1, 0, 0), (1, 0, 1), (1, 1, 0)]

    def finish(half):
        for way in range(2):
            ring(way, half, 2).wait_recv()
            out_buf[8 * half + 7 - way] += ring_buf[way, half, 2]
        for what in handed[half]:
            hand_over(*what).start()

    def emit(d, bar, total):
        pack(d["out"], bar, total)
        acc[...] += d["load"][...] * bar

    def scenario(pair, k):
        owner_x, owner_z = owner(pair, k)
        s = owner_x * Z + owner_z
        return dict(
            load=load_v.at[pair, k], z=z_v.at[pair, k], cot=cot_v.at[pair, k], out=out_buf.at[pair, k],
            first=first_ref[s], r0=start_ref[pl.ds(s, 1), :],
        )

    def share(buf, peer, me, stage):
        return [
            pltpu.make_async_remote_copy(
                src_ref=buf.at[me],
                dst_ref=buf.at[me],
                send_sem=s_send.at[stage, k],
                recv_sem=s_recv.at[stage, k],
                device_id=peer(k),
                device_id_type=MESH,
            )
            for k in range(1, SIXTEEN)
        ]

    stage_plane = share(s_plane, plane_peer, y * X + x, 0)
    stage_line = share(s_line, line_peer, core * Z + z, 1)

    @pl.loop(0, 4)
    def _(group):
        for j in range(4):
            for copy in fetches(4 * group + j):
                copy.wait()
        items = [scenario(4 * group + j, k) for j in range(4) for k in range(2)]
        adjoint_of(items, stress_col, log_paths, emit)

        @pl.when(group == 0)
        def _():
            pl.semaphore_wait(barrier, 2 * (SIXTEEN - 1))

        @pl.when(group == 3)
        def _():
            part = jnp.sum(jnp.where(eye, jnp.sum(acc[...], axis=1, keepdims=True), 0.0), axis=0, keepdims=True)
            s_plane[y * X + x, :, 0:NR] = jnp.broadcast_to(part, (8, NR))
            s_plane[y * X + x, :, NR:128] = jnp.zeros((8, 128 - NR), f32)
            for copy in stage_plane:
                copy.start()

        half = group // 2
        for j in range(2):
            step = 2 * (group % 2) + j
            for way in range(2):

                @pl.when(step >= 2)
                def _():
                    ring(way, half, step - 2).wait_recv()
                    out_buf[8 * half + 2 * step + way] += ring_buf[way, half, step - 2]

                @pl.when(step < 3)
                def _():
                    ring(way, half, step).start()

        @pl.when(group == 2)
        def _():
            finish(0)

    finish(1)

    for copy in stage_plane:
        copy.wait_recv()
    s_line[core * Z + z] = jnp.sum(s_plane[...], axis=0)
    for copy in stage_line:
        copy.start()

    lam = scaled_loadings(load_v[14, 1], stress_col, first_ref[path], rows)
    lh, ll = split(lam)
    cov = (dot_nt(lh, lh) + dot_nt(lh, ll) + dot_nt(ll, lh)) * (LN2 * LN2)
    r0 = start_ref[pl.ds(path, 1), :]

    for what in handed[0] + handed[1]:
        hand_over(*what).wait_recv()
    bar, total = unpack(out_buf[14, 1] + jnp.sum(z_buf[...], axis=0))
    out[0:NR, 0:NR] = stress_col * bar
    through = jnp.sum(jnp.where(rows >= cols, cov, 0.0) * total, axis=0, keepdims=True)
    direct = jnp.sum(jnp.where(eye, total, 0.0), axis=0, keepdims=True)
    out[80:81, 0:NR] = direct / r0 + through * (100.0 / ((100.0 + r0) * (100.0 + r0)))

    results = [
        pltpu.make_async_copy(out.at[part], out_hbm.at[part], out_sem.at[i])
        for i, part in enumerate((pl.ds(0, 88), pl.ds(88, 8)))
    ]
    results[0].start()

    for copy in stage_line:
        copy.wait_recv()
    out[88:96] = jnp.sum(s_line[...], axis=0)
    results[1].start()

    for half in range(2):
        for way in range(2):
            for step in range(3):
                ring(way, half, step).wait_send()
    for what in handed[0] + handed[1]:
        hand_over(*what).wait_send()
    for copy in stage_plane + stage_line:
        copy.wait_send()
    for copy in results:
        copy.wait()


def hand_on(packed, rate_out, vol_out, stress_out):
    rate_out[...] = packed[80:81, 0:NR]
    vol_out[0] = packed[0:NR, 0:NR]
    stress_out[...] = packed[88:89, 0:NR]


def body(start_rates, loadings, stress, increments, cotangent, first_active):
    log_paths = math.log2(WIDTH * X * Z)
    vmem = pl.BlockSpec(memory_space=pltpu.VMEM)
    anywhere = pl.BlockSpec(memory_space=pl.ANY)
    dma = pltpu.SemaphoreType.DMA
    summed = pl.pallas_call(
        lambda *refs: kernel(log_paths, *refs),
        out_shape=jax.ShapeDtypeStruct((96, 128), f32),
        in_specs=[anywhere] * 6,
        out_specs=anywhere,
        scratch_shapes=[
            pltpu.VMEM((1, NR), f32),
            pltpu.SMEM((2 * PAIRS,), jnp.int32),
            pltpu.VMEM((2 * PAIRS, NR), f32),
            pltpu.VMEM((96, 128), f32),
            pltpu.VMEM((PAIRS, 2, NR, NR), f32),
            pltpu.VMEM((PAIRS, 2, 2, NR, WIDTH), bf16),
            pltpu.VMEM((PAIRS, 2, NR, WIDTH), f32),
            pltpu.VMEM((PAIRS, 2, PACKED, 128), f32),
            pltpu.VMEM((2, 2, 3, 2, PACKED, 128), f32),
            pltpu.VMEM((Z - 1, PACKED, 128), f32),
            pltpu.VMEM((NR, NR), f32),
            pltpu.VMEM((SIXTEEN, 8, 128), f32),
            pltpu.VMEM((SIXTEEN, 8, 128), f32),
            dma((3,)),
            dma((2,)),
            dma((3, PAIRS, 2)),
            dma((2, 2, 3)),
            dma((2, 2, 3)),
            dma((Z - 1,)),
            dma((Z - 1,)),
            dma((2, SIXTEEN)),
            dma((2, SIXTEEN)),
        ],
        compiler_params=pltpu.CompilerParams(
            collective_id=0, has_side_effects=True, vmem_limit_bytes=56 * 2**20
        ),
        name="adjoint",
    )(
        stress[None],
        first_active,
        start_rates,
        loadings.reshape(X, Z, NR, NR),
        increments.reshape(X, Z, 2, NR, WIDTH),
        cotangent.reshape(X, Z, NR, WIDTH),
    )
    rate, vol, stress_gradient = pl.pallas_call(
        hand_on,
        out_shape=(
            jax.ShapeDtypeStruct((1, NR), f32),
            jax.ShapeDtypeStruct((1, NR, NR), f32),
            jax.ShapeDtypeStruct((1, NR), f32),
        ),
        in_specs=[vmem],
        out_specs=(vmem, vmem, vmem),
        name="results",
    )(summed)
    return rate, vol, stress_gradient[0]


def solution(mesh):
    return jax.shard_map(
        body,
        mesh=mesh,
        in_specs=(
            P("grp", None),
            P("grp", None, None),
            P(),
            P("grp", None, None, "path"),
            P("grp", None, "path"),
            P("grp"),
        ),
        out_specs=(P(("grp", "path"), None), P(("grp", "path"), None, None), P()),
        check_vma=False,
    )
```

```python
import math

import jax
import jax.numpy as jnp
from jax import lax
from jax.experimental import pallas as pl
from jax.experimental.pallas import tpu as pltpu
from jax.sharding import PartitionSpec as P

NR = 80
WIDTH = 256
X, Z = 4, 8
Y, CORES = 4, 2
SIXTEEN = X * Y
PAIRS = 16
PACKED = 56
LN2 = math.log(2.0)
LOG2E = 1.0 / LN2
bf16 = jnp.bfloat16
f32 = jnp.float32
MESH = pl.DeviceIdType.MESH


def dot(a, b):
    return jnp.dot(a, b, preferred_element_type=f32)


def dot_nt(a, b):
    return lax.dot_general(a, b, (((1,), (1,)), ((), ())), preferred_element_type=f32)


def split(value):
    high = value.astype(bf16)
    return high, (value - high.astype(f32)).astype(bf16)


def index_masks():
    rows = lax.broadcasted_iota(jnp.int32, (NR, NR), 0)
    cols = lax.broadcasted_iota(jnp.int32, (NR, NR), 1)
    return rows, cols


STEPS = {(0, 0): 0, (0, 1): 1, (1, 0): 2, (0, 2): 3, (1, 1): 4, (0, 3): 5, (1, 2): 6, (1, 3): 7}


def place(pair, k, x):
    at, way = pair // 2, pair % 2
    half = (at + 1) % 2 - (7 - at) // 7 + at // 7
    step = (at + 1 - 2 * half) // 2
    reach = 2 - (step + 1) // 2
    side = lax.rem(step + way, 2)
    hops = 3 - 2 * half - side if k else 4 + 2 * half + side
    return lax.rem(x + reach * (1 - way) + (X - reach) * way, X), hops


def scaled_loadings(load, stress_col, first, rows):
    return load * jnp.where(rows >= first, stress_col * LOG2E, 0.0)


def forward(items, held, slot, masks, stress_col, log_paths):
    rows, cols = index_masks()
    eye = rows == cols
    for k, d in enumerate(items):
        yield
        d["lam"] = scaled_loadings(d["load"][...], stress_col, d["first"], rows)
        d["lh"], d["ll"] = split(d["lam"])
        held["lam"][slot, k] = d["lam"]
    for d in items:
        yield
        d["cov"] = dot_nt(d["lh"], d["lh"])
    for k, d in enumerate(items):
        yield
        drift = d["cov"] * masks[0]
        r0 = d["r0"]
        accrual = r0 / (100.0 + r0)
        half = jnp.sum(d["lam"] * d["lam"], axis=1, keepdims=True) * (-0.5 * LN2)
        c1 = jnp.sum(drift * accrual + jnp.where(eye, jnp.log2(r0), 0.0), axis=1, keepdims=True)
        d["c1"] = half + c1 - math.log2(100.0)
        d["c2"] = half + (math.log2(100.0) - log_paths)
        d["left"] = jnp.concatenate([d["lh"], d["ll"], drift.astype(bf16)], axis=1)
        held["back"][slot, k] = (d["cov"] * masks[1]).astype(bf16)
    for d in items:
        yield
        z1 = d["z"][0]
        d["e1"] = dot(d["left"][:, : 2 * NR], jnp.concatenate([z1, z1], axis=0))
    for k, d in enumerate(items):
        yield
        mid = jnp.exp2(d["e1"] + d["c1"])
        inverse = 1.0 / (1.0 + mid)
        accrual = mid * inverse
        d["mid"], d["a"] = mid, accrual.astype(bf16)
        held["a"][slot, k] = d["a"]
        held["slope"][slot, k] = accrual * inverse
    for d in items:
        yield
        z2 = d["z"][1]
        d["e2"] = dot(d["left"], jnp.concatenate([z2, z2, d["a"]], axis=0))
    for k, d in enumerate(items):
        yield
        held["g2"][slot, k] = d["mid"] * jnp.exp2(d["e2"] + d["c2"]) * d["cot"][...]


def adjoint(items, held, slot, emit):
    rows, cols = index_masks()
    low = rows >= cols
    ones = jnp.ones((16, WIDTH), bf16)
    gap = jnp.zeros((32, WIDTH), bf16)
    for k, d in enumerate(items):
        yield
        d["g2"] = held["g2"][slot, k]
        d["g2h"], d["g2l"] = split(d["g2"])
    for k, d in enumerate(items):
        yield
        d["da"] = dot(held["back"][slot, k], d["g2h"])
    for k, d in enumerate(items):
        yield
        right = jnp.concatenate([d["z"][1], ones, gap, held["a"][slot, k]], axis=0)
        d["sums2"] = dot_nt(jnp.concatenate([d["g2h"], d["g2l"]], axis=0), right)
    for k, d in enumerate(items):
        yield
        g1h, g1l = split(d["g2"] + held["slope"][slot, k] * d["da"])
        right = jnp.concatenate([d["z"][0], ones], axis=0)
        d["sums1"] = dot_nt(jnp.concatenate([g1h, g1l], axis=0), right)
    for k, d in enumerate(items):
        yield
        lam = held["lam"][slot, k]
        lh, ll = split(lam)
        sum1 = d["sums1"][:NR] + d["sums1"][NR:]
        sum2 = d["sums2"][:NR, :128] + d["sums2"][NR:, :128]
        outer = d["sums2"][:NR, 128:208] + d["sums2"][NR:, 128:208]
        total1, total2 = sum1[:, NR : NR + 1], sum2[:, NR : NR + 1]
        bar_cov = jnp.where(low, outer + total1 * (d["r0"] / (100.0 + d["r0"])), 0.0)
        mh, ml = split((bar_cov + bar_cov.T) * LN2)
        through = dot(jnp.concatenate([mh, ml, mh], axis=1), jnp.concatenate([lh, lh, ll], axis=0))
        bar = sum1[:, :NR] + sum2[:, :NR] + through - ((total1 + total2) * LN2) * lam
        emit(d, jnp.where(rows >= d["first"], bar, 0.0), total1)


def interleaved(*parts):
    parts = list(parts)
    while parts:
        for part in list(parts):
            if next(part, parts) is parts:
                parts.remove(part)


def pack(ref, bar, total):
    ref[:, 0:NR] = bar[:PACKED]
    ref[:, NR : NR + 1] = total[:PACKED]
    rest = jnp.concatenate([bar[PACKED:], total[PACKED:]], axis=1)
    ref[0:24, 81:128] = rest[:, 0:47]
    ref[24:48, 81:115] = rest[:, 47:81]
    ref[24:48, 115:128] = jnp.zeros((24, 13), f32)
    ref[48:56, 81:128] = jnp.zeros((8, 47), f32)


def unpack(value):
    rest = jnp.concatenate([value[0:24, 81:128], value[24:48, 81:115]], axis=1)
    bar = jnp.concatenate([value[:, 0:NR], rest[:, 0:NR]], axis=0)
    total = jnp.concatenate([value[:, NR : NR + 1], rest[:, NR : NR + 1]], axis=0)
    return bar, total


def kernel(
    log_paths,
    stress_hbm, first_hbm, start_hbm, load_hbm, z_hbm, cot_hbm,
    out_hbm,
    stress_ref, first_ref, start_ref, out,
    load_v, z_v, cot_v, out_buf, ring_buf, z_buf, acc, s_plane, s_line,
    h_lam, h_back, h_a, h_slope, h_g2,
    small_sem, out_sem, in_sem, ring_send, ring_recv, z_send, z_recv, s_send, s_recv,
):
    g = lax.axis_index("grp")
    path = lax.axis_index("path")
    x, z = path // Z, lax.rem(path, Z)

    def owner(pair, k):
        owner_x, hops = place(pair, k, x)
        return owner_x, lax.rem(z + hops, Z)

    def fetches(pair):
        return [
            pltpu.make_async_copy(hbm.at[owner(pair, k)], vmem.at[pair, k], in_sem.at[i, pair, k])
            for k in range(2)
            for i, (hbm, vmem) in enumerate(((load_hbm, load_v), (z_hbm, z_v), (cot_hbm, cot_v)))
        ]

    small = [
        pltpu.make_async_copy(hbm, here, small_sem.at[i])
        for i, (hbm, here) in enumerate(((stress_hbm, stress_ref), (first_hbm, first_ref), (start_hbm, start_ref)))
    ]
    for copy in small:
        copy.start()

    @pl.loop(0, 4)
    def _(pair):
        for copy in fetches(pair):
            copy.start()

    def x_peer(k):
        return (g, lax.rem(x + k, X) * Z + z)

    def z_peer(k):
        return (g, x * Z + lax.rem(z + k, Z))

    y, core = g // CORES, lax.rem(g, CORES)

    def plane_peer(k):
        return (lax.rem(y + k // X, Y) * CORES + core, lax.rem(x + k % X, X) * Z + z)

    def line_peer(k):
        return (y * CORES + lax.rem(core + k // Z, CORES), x * Z + lax.rem(z + k % Z, Z))

    barrier = pltpu.get_barrier_semaphore()
    for k in range(1, SIXTEEN):
        for peer in (plane_peer, line_peer):
            pl.semaphore_signal(barrier, inc=1, device_id=peer(k), device_id_type=MESH)

    @pl.loop(4, PAIRS)
    def _(pair):
        for copy in fetches(pair):
            copy.start()

    for copy in small:
        copy.wait()
    rows, cols = index_masks()
    eye = rows == cols
    stress_col = jnp.sum(jnp.where(eye, stress_ref[...], 0.0), axis=1, keepdims=True)
    acc[...] = jnp.zeros_like(acc)

    def ring(way, half, step):
        return pltpu.make_async_remote_copy(
            src_ref=out_buf.at[2 * STEPS[half, step] + way],
            dst_ref=ring_buf.at[way, half, step],
            send_sem=ring_send.at[way, half, step],
            recv_sem=ring_recv.at[way, half, step],
            device_id=x_peer(X - 1 if way else 1),
            device_id_type=MESH,
        )

    def hand_over(half, side, k):
        hops = 3 - 2 * half - side if k else 4 + 2 * half + side
        return pltpu.make_async_remote_copy(
            src_ref=out_buf.at[2 * STEPS[half, 3] + 1 - side, k],
            dst_ref=z_buf.at[hops - 1],
            send_sem=z_send.at[hops - 1],
            recv_sem=z_recv.at[hops - 1],
            device_id=z_peer(hops),
            device_id_type=MESH,
        )

    handed = [(0, side, k) for side in range(2) for k in range(2)], [(1, 0, 0), (1, 0, 1), (1, 1, 0)]

    def finish(half):
        for way in range(2):
            ring(way, half, 2).wait_recv()
            out_buf[2 * STEPS[half, 3] + 1 - way] += ring_buf[way, half, 2]
        for what in handed[half]:
            hand_over(*what).start()

    def emit(d, bar, total):
        pack(d["out"], bar, total)
        acc[...] += d["load"][...] * bar

    def scenario(pair, k):
        owner_x, owner_z = owner(pair, k)
        s = owner_x * Z + owner_z
        return dict(
            load=load_v.at[pair, k], z=z_v.at[pair, k], cot=cot_v.at[pair, k], out=out_buf.at[pair, k],
            first=first_ref[s], r0=start_ref[pl.ds(s, 1), :],
        )

    def share(buf, peer, me, stage):
        return [
            pltpu.make_async_remote_copy(
                src_ref=buf.at[me],
                dst_ref=buf.at[me],
                send_sem=s_send.at[stage, k],
                recv_sem=s_recv.at[stage, k],
                device_id=peer(k),
                device_id_type=MESH,
            )
            for k in range(1, SIXTEEN)
        ]

    stage_plane = share(s_plane, plane_peer, y * X + x, 0)
    stage_line = share(s_line, line_peer, core * Z + z, 1)

    masks = (jnp.where(rows >= cols, LN2, 0.0), jnp.where(rows <= cols, LN2 * LN2, 0.0))
    held = dict(lam=h_lam, back=h_back, a=h_a, slope=h_slope, g2=h_g2)

    def items(group):
        return [scenario(4 * group + j, k) for j in range(4) for k in range(2)]

    def start(group, slot):
        for j in range(4):
            for copy in fetches(4 * group + j):
                copy.wait()
        return forward(items(group), held, slot, masks, stress_col, log_paths)

    def send(half, step):
        for way in range(2):
            ring(way, half, step).start()

    def take(half, step):
        for way in range(2):
            ring(way, half, step - 2).wait_recv()
            out_buf[2 * STEPS[half, step] + way] += ring_buf[way, half, step - 2]

    interleaved(start(0, 0))

    @pl.loop(1, 4)
    def _(group):
        slot = lax.rem(group, 2)
        ahead = start(group, slot)
        interleaved(adjoint(items(group - 1), held, 1 - slot, emit), ahead)

        @pl.when(group == 1)
        def _():
            pl.semaphore_wait(barrier, 2 * (SIXTEEN - 1))
            send(0, 0)
            send(0, 1)

        @pl.when(group == 2)
        def _():
            send(1, 0)

        @pl.when(group == 3)
        def _():
            take(0, 2)
            send(0, 2)
            send(1, 1)

    interleaved(adjoint(items(3), held, 1, emit))
    part = jnp.sum(jnp.where(eye, jnp.sum(acc[...], axis=1, keepdims=True), 0.0), axis=0, keepdims=True)
    s_plane[y * X + x, :, 0:NR] = jnp.broadcast_to(part, (8, NR))
    s_plane[y * X + x, :, NR:128] = jnp.zeros((8, 128 - NR), f32)
    for copy in stage_plane:
        copy.start()
    take(1, 2)
    send(1, 2)
    take(0, 3)
    finish(0)

    for copy in stage_plane:
        copy.wait_recv()
    s_line[core * Z + z] = jnp.sum(s_plane[...], axis=0)
    for copy in stage_line:
        copy.start()

    take(1, 3)
    finish(1)

    lam = scaled_loadings(load_v[14, 1], stress_col, first_ref[path], rows)
    lh, ll = split(lam)
    cov = (dot_nt(lh, lh) + dot_nt(lh, ll) + dot_nt(ll, lh)) * (LN2 * LN2)
    r0 = start_ref[pl.ds(path, 1), :]

    for what in handed[0] + handed[1]:
        hand_over(*what).wait_recv()
    bar, total = unpack(out_buf[14, 1] + jnp.sum(z_buf[...], axis=0))
    out[0:NR, 0:NR] = stress_col * bar
    through = jnp.sum(jnp.where(rows >= cols, cov, 0.0) * total, axis=0, keepdims=True)
    direct = jnp.sum(jnp.where(eye, total, 0.0), axis=0, keepdims=True)
    out[80:81, 0:NR] = direct / r0 + through * (100.0 / ((100.0 + r0) * (100.0 + r0)))

    results = [
        pltpu.make_async_copy(out.at[part], out_hbm.at[part], out_sem.at[i])
        for i, part in enumerate((pl.ds(0, 88), pl.ds(88, 8)))
    ]
    results[0].start()

    for half in range(2):
        for way in range(2):
            for step in range(3):
                ring(way, half, step).wait_send()
    for what in handed[0] + handed[1]:
        hand_over(*what).wait_send()
    for copy in stage_plane + stage_line:
        copy.wait_send()
    for copy in stage_line:
        copy.wait_recv()
    out[88:96] = jnp.sum(s_line[...], axis=0)
    results[1].start()

    for copy in results:
        copy.wait()


def hand_on(packed, rate_out, vol_out, stress_out):
    rate_out[...] = packed[80:81, 0:NR]
    vol_out[0] = packed[0:NR, 0:NR]
    stress_out[...] = packed[88:89, 0:NR]


def body(start_rates, loadings, stress, increments, cotangent, first_active):
    log_paths = math.log2(WIDTH * X * Z)
    vmem = pl.BlockSpec(memory_space=pltpu.VMEM)
    anywhere = pl.BlockSpec(memory_space=pl.ANY)
    dma = pltpu.SemaphoreType.DMA
    summed = pl.pallas_call(
        lambda *refs: kernel(log_paths, *refs),
        out_shape=jax.ShapeDtypeStruct((96, 128), f32),
        in_specs=[anywhere] * 6,
        out_specs=anywhere,
        scratch_shapes=[
            pltpu.VMEM((1, NR), f32),
            pltpu.SMEM((2 * PAIRS,), jnp.int32),
            pltpu.VMEM((2 * PAIRS, NR), f32),
            pltpu.VMEM((96, 128), f32),
            pltpu.VMEM((PAIRS, 2, NR, NR), f32),
            pltpu.VMEM((PAIRS, 2, 2, NR, WIDTH), bf16),
            pltpu.VMEM((PAIRS, 2, NR, WIDTH), f32),
            pltpu.VMEM((PAIRS, 2, PACKED, 128), f32),
            pltpu.VMEM((2, 2, 3, 2, PACKED, 128), f32),
            pltpu.VMEM((Z - 1, PACKED, 128), f32),
            pltpu.VMEM((NR, NR), f32),
            pltpu.VMEM((SIXTEEN, 8, 128), f32),
            pltpu.VMEM((SIXTEEN, 8, 128), f32),
            pltpu.VMEM((2, 8, NR, NR), f32),
            pltpu.VMEM((2, 8, NR, NR), bf16),
            pltpu.VMEM((2, 8, NR, WIDTH), bf16),
            pltpu.VMEM((2, 8, NR, WIDTH), f32),
            pltpu.VMEM((2, 8, NR, WIDTH), f32),
            dma((3,)),
            dma((2,)),
            dma((3, PAIRS, 2)),
            dma((2, 2, 3)),
            dma((2, 2, 3)),
            dma((Z - 1,)),
            dma((Z - 1,)),
            dma((2, SIXTEEN)),
            dma((2, SIXTEEN)),
        ],
        compiler_params=pltpu.CompilerParams(
            collective_id=0, has_side_effects=True, vmem_limit_bytes=56 * 2**20
        ),
        name="adjoint",
    )(
        stress[None],
        first_active,
        start_rates,
        loadings.reshape(X, Z, NR, NR),
        increments.reshape(X, Z, 2, NR, WIDTH),
        cotangent.reshape(X, Z, NR, WIDTH),
    )
    rate, vol, stress_gradient = pl.pallas_call(
        hand_on,
        out_shape=(
            jax.ShapeDtypeStruct((1, NR), f32),
            jax.ShapeDtypeStruct((1, NR, NR), f32),
            jax.ShapeDtypeStruct((1, NR), f32),
        ),
        in_specs=[vmem],
        out_specs=(vmem, vmem, vmem),
        name="results",
    )(summed)
    return rate, vol, stress_gradient[0]


def solution(mesh):
    return jax.shard_map(
        body,
        mesh=mesh,
        in_specs=(
            P("grp", None),
            P("grp", None, None),
            P(),
            P("grp", None, None, "path"),
            P("grp", None, "path"),
            P("grp"),
        ),
        out_specs=(P(("grp", "path"), None), P(("grp", "path"), None, None), P()),
        check_vma=False,
    )
```

```python
import math

import jax
import jax.numpy as jnp
from jax import lax
from jax.experimental import pallas as pl
from jax.experimental.pallas import tpu as pltpu
from jax.sharding import PartitionSpec as P

NR = 80
WIDTH = 256
X, Z = 4, 8
Y, CORES = 4, 2
SIXTEEN = X * Y
PAIRS = 16
PACKED = 56
LN2 = math.log(2.0)
LOG2E = 1.0 / LN2
bf16 = jnp.bfloat16
f32 = jnp.float32
MESH = pl.DeviceIdType.MESH


def dot(a, b):
    return jnp.dot(a, b, preferred_element_type=f32)


def dot_nt(a, b):
    return lax.dot_general(a, b, (((1,), (1,)), ((), ())), preferred_element_type=f32)


def split(value):
    high = value.astype(bf16)
    return high, (value - high.astype(f32)).astype(bf16)


def index_masks():
    rows = lax.broadcasted_iota(jnp.int32, (NR, NR), 0)
    cols = lax.broadcasted_iota(jnp.int32, (NR, NR), 1)
    return rows, cols


STEPS = {(0, 0): 0, (0, 1): 1, (1, 0): 2, (0, 2): 3, (1, 1): 4, (0, 3): 5, (1, 2): 6, (1, 3): 7}


def place(pair, k, x):
    at, way = pair // 2, pair % 2
    half = (at + 1) % 2 - (7 - at) // 7 + at // 7
    step = (at + 1 - 2 * half) // 2
    reach = 2 - (step + 1) // 2
    side = lax.rem(step + way, 2)
    hops = 3 - 2 * half - side if k else 4 + 2 * half + side
    return lax.rem(x + reach * (1 - way) + (X - reach) * way, X), hops


def scaled_loadings(load, stress_col, first, rows):
    return load * jnp.where(rows >= first, stress_col * LOG2E, 0.0)


def forward(items, held, slot, masks, stress_col, log_paths):
    rows, cols = index_masks()
    eye = rows == cols
    for k, d in enumerate(items):
        yield
        d["lam"] = scaled_loadings(d["load"][...], stress_col, d["first"], rows)
        d["lh"], d["ll"] = split(d["lam"])
        held["lam"][slot, k] = d["lam"]
    for d in items:
        yield
        d["cov"] = dot_nt(d["lh"], d["lh"])
    for k, d in enumerate(items):
        yield
        drift = d["cov"] * masks[0]
        r0 = d["r0"]
        accrual = r0 / (100.0 + r0)
        half = jnp.sum(d["lam"] * d["lam"], axis=1, keepdims=True) * (-0.5 * LN2)
        c1 = jnp.sum(drift * accrual + jnp.where(eye, jnp.log2(r0), 0.0), axis=1, keepdims=True)
        d["c1"] = half + c1 - math.log2(100.0)
        d["c2"] = half + (math.log2(100.0) - log_paths)
        d["left"] = jnp.concatenate([d["lh"], d["ll"], drift.astype(bf16)], axis=1)
        held["back"][slot, k] = (d["cov"] * masks[1]).astype(bf16)
    for d in items:
        yield
        z1 = d["z"][0]
        d["e1"] = dot(d["left"][:, : 2 * NR], jnp.concatenate([z1, z1], axis=0))
    for k, d in enumerate(items):
        yield
        mid = jnp.exp2(d["e1"] + d["c1"])
        inverse = 1.0 / (1.0 + mid)
        accrual = mid * inverse
        d["mid"], d["a"] = mid, accrual.astype(bf16)
        held["a"][slot, k] = d["a"]
        held["slope"][slot, k] = accrual * inverse
    for d in items:
        yield
        z2 = d["z"][1]
        d["e2"] = dot(d["left"], jnp.concatenate([z2, z2, d["a"]], axis=0))
    for k, d in enumerate(items):
        yield
        held["g2"][slot, k] = d["mid"] * jnp.exp2(d["e2"] + d["c2"]) * d["cot"][...]


def adjoint(items, held, slot, emit):
    rows, cols = index_masks()
    low = rows >= cols
    ones = jnp.ones((16, WIDTH), bf16)
    gap = jnp.zeros((32, WIDTH), bf16)
    for k, d in enumerate(items):
        yield
        d["g2"] = held["g2"][slot, k]
        d["g2h"], d["g2l"] = split(d["g2"])
    for k, d in enumerate(items):
        yield
        d["da"] = dot(held["back"][slot, k], d["g2h"])
    for k, d in enumerate(items):
        yield
        right = jnp.concatenate([d["z"][1], ones, gap, held["a"][slot, k]], axis=0)
        d["sums2"] = dot_nt(jnp.concatenate([d["g2h"], d["g2l"]], axis=0), right)
    for k, d in enumerate(items):
        yield
        g1h, g1l = split(d["g2"] + held["slope"][slot, k] * d["da"])
        right = jnp.concatenate([d["z"][0], ones], axis=0)
        d["sums1"] = dot_nt(jnp.concatenate([g1h, g1l], axis=0), right)
    for k, d in enumerate(items):
        yield
        lam = held["lam"][slot, k]
        lh, ll = split(lam)
        sum1 = d["sums1"][:NR] + d["sums1"][NR:]
        sum2 = d["sums2"][:NR, :128] + d["sums2"][NR:, :128]
        outer = d["sums2"][:NR, 128:208] + d["sums2"][NR:, 128:208]
        total1, total2 = sum1[:, NR : NR + 1], sum2[:, NR : NR + 1]
        bar_cov = jnp.where(low, outer + total1 * (d["r0"] / (100.0 + d["r0"])), 0.0)
        mh, ml = split((bar_cov + bar_cov.T) * LN2)
        through = dot(jnp.concatenate([mh, ml, mh], axis=1), jnp.concatenate([lh, lh, ll], axis=0))
        bar = sum1[:, :NR] + sum2[:, :NR] + through - ((total1 + total2) * LN2) * lam
        emit(d, jnp.where(rows >= d["first"], bar, 0.0), total1)


def interleaved(*parts):
    parts = list(parts)
    while parts:
        for part in list(parts):
            if next(part, parts) is parts:
                parts.remove(part)


def wait_for(ref, sem):
    pltpu.make_async_copy(ref, ref, sem).wait()


def pack(ref, bar, total):
    ref[:, 0:NR] = bar[:PACKED]
    ref[:, NR : NR + 1] = total[:PACKED]
    rest = jnp.concatenate([bar[PACKED:], total[PACKED:]], axis=1)
    ref[0:24, 81:128] = rest[:, 0:47]
    ref[24:48, 81:115] = rest[:, 47:81]
    ref[24:48, 115:128] = jnp.zeros((24, 13), f32)
    ref[48:56, 81:128] = jnp.zeros((8, 47), f32)


def unpack(value):
    rest = jnp.concatenate([value[0:24, 81:128], value[24:48, 81:115]], axis=1)
    bar = jnp.concatenate([value[:, 0:NR], rest[:, 0:NR]], axis=0)
    total = jnp.concatenate([value[:, NR : NR + 1], rest[:, NR : NR + 1]], axis=0)
    return bar, total


def kernel(
    log_paths,
    stress_hbm, first_hbm, start_hbm, load_hbm, z_hbm, cot_hbm,
    out_hbm,
    stress_ref, first_ref, start_ref, out,
    load_v, z_v, cot_v, out_buf, ring_buf, z_buf, acc, s_plane, s_line,
    h_lam, h_back, h_a, h_slope, h_g2,
    small_sem, out_sem, in_sem, ring_send, ring_recv, z_send, z_recv, s_send, s_recv,
):
    g = lax.axis_index("grp")
    path = lax.axis_index("path")
    x, z = path // Z, lax.rem(path, Z)

    def owner(pair, k):
        owner_x, hops = place(pair, k, x)
        return owner_x, lax.rem(z + hops, Z)

    def fetches(pair):
        return [
            pltpu.make_async_copy(hbm.at[owner(pair, k)], vmem.at[pair, k], in_sem.at[i, pair // 4])
            for k in range(2)
            for i, (hbm, vmem) in enumerate(((load_hbm, load_v), (z_hbm, z_v), (cot_hbm, cot_v)))
        ]

    small = [
        pltpu.make_async_copy(hbm, here, small_sem.at[i])
        for i, (hbm, here) in enumerate(((stress_hbm, stress_ref), (first_hbm, first_ref), (start_hbm, start_ref)))
    ]
    for copy in small:
        copy.start()

    @pl.loop(0, 4)
    def _(pair):
        for copy in fetches(pair):
            copy.start()

    def x_peer(k):
        return (g, lax.rem(x + k, X) * Z + z)

    def z_peer(k):
        return (g, x * Z + lax.rem(z + k, Z))

    y, core = g // CORES, lax.rem(g, CORES)

    def plane_peer(k):
        return (lax.rem(y + k // X, Y) * CORES + core, lax.rem(x + k % X, X) * Z + z)

    def line_peer(k):
        return (y * CORES + lax.rem(core + k // Z, CORES), x * Z + lax.rem(z + k % Z, Z))

    barrier = pltpu.get_barrier_semaphore()
    for k in range(1, SIXTEEN):
        for peer in (plane_peer, line_peer):
            pl.semaphore_signal(barrier, inc=1, device_id=peer(k), device_id_type=MESH)

    @pl.loop(4, PAIRS)
    def _(pair):
        for copy in fetches(pair):
            copy.start()

    for copy in small:
        copy.wait()
    rows, cols = index_masks()
    eye = rows == cols
    stress_col = jnp.sum(jnp.where(eye, stress_ref[...], 0.0), axis=1, keepdims=True)
    acc[...] = jnp.zeros_like(acc)

    def ring(way, half, step):
        return pltpu.make_async_remote_copy(
            src_ref=out_buf.at[2 * STEPS[half, step] + way],
            dst_ref=ring_buf.at[half, step, way],
            send_sem=ring_send,
            recv_sem=ring_recv.at[half, step],
            device_id=x_peer(X - 1 if way else 1),
            device_id_type=MESH,
        )

    def hand_over(half, side, k):
        hops = 3 - 2 * half - side if k else 4 + 2 * half + side
        return pltpu.make_async_remote_copy(
            src_ref=out_buf.at[2 * STEPS[half, 3] + 1 - side, k],
            dst_ref=z_buf.at[hops - 1],
            send_sem=z_send,
            recv_sem=z_recv,
            device_id=z_peer(hops),
            device_id_type=MESH,
        )

    handed = [(0, side, k) for side in range(2) for k in range(2)], [(1, 0, 0), (1, 0, 1), (1, 1, 0)]

    def arrived(half, step):
        wait_for(ring_buf.at[half, step], ring_recv.at[half, step])

    def finish(half):
        arrived(half, 2)
        for way in range(2):
            out_buf[2 * STEPS[half, 3] + 1 - way] += ring_buf[half, 2, way]
        for what in handed[half]:
            hand_over(*what).start()

    def emit(d, bar, total):
        pack(d["out"], bar, total)
        acc[...] += d["load"][...] * bar

    def scenario(pair, k):
        owner_x, owner_z = owner(pair, k)
        s = owner_x * Z + owner_z
        return dict(
            load=load_v.at[pair, k], z=z_v.at[pair, k], cot=cot_v.at[pair, k], out=out_buf.at[pair, k],
            first=first_ref[s], r0=start_ref[pl.ds(s, 1), :],
        )

    def share(buf, peer, me, stage):
        return [
            pltpu.make_async_remote_copy(
                src_ref=buf.at[me],
                dst_ref=buf.at[me],
                send_sem=s_send.at[stage],
                recv_sem=s_recv.at[stage],
                device_id=peer(k),
                device_id_type=MESH,
            )
            for k in range(1, SIXTEEN)
        ]

    stage_plane = share(s_plane, plane_peer, y * X + x, 0)
    stage_line = share(s_line, line_peer, core * Z + z, 1)

    masks = (jnp.where(rows >= cols, LN2, 0.0), jnp.where(rows <= cols, LN2 * LN2, 0.0))
    held = dict(lam=h_lam, back=h_back, a=h_a, slope=h_slope, g2=h_g2)

    def items(group):
        return [scenario(4 * group + j, k) for j in range(4) for k in range(2)]

    def start(group, slot):
        blocks = pl.ds(4 * group, 4)
        for i, vmem in enumerate((load_v, z_v, cot_v)):
            wait_for(vmem.at[blocks], in_sem.at[i, group])
        return forward(items(group), held, slot, masks, stress_col, log_paths)

    def send(half, step):
        for way in range(2):
            ring(way, half, step).start()

    def take(half, step):
        arrived(half, step - 2)
        for way in range(2):
            out_buf[2 * STEPS[half, step] + way] += ring_buf[half, step - 2, way]

    interleaved(start(0, 0))

    @pl.loop(1, 4)
    def _(group):
        slot = lax.rem(group, 2)
        ahead = start(group, slot)
        interleaved(adjoint(items(group - 1), held, 1 - slot, emit), ahead)

        @pl.when(group == 1)
        def _():
            pl.semaphore_wait(barrier, 2 * (SIXTEEN - 1))
            send(0, 0)
            send(0, 1)

        @pl.when(group == 2)
        def _():
            send(1, 0)

        @pl.when(group == 3)
        def _():
            take(0, 2)
            send(0, 2)
            send(1, 1)

    interleaved(adjoint(items(3), held, 1, emit))
    part = jnp.sum(jnp.where(eye, jnp.sum(acc[...], axis=1, keepdims=True), 0.0), axis=0, keepdims=True)
    s_plane[y * X + x, :, 0:NR] = jnp.broadcast_to(part, (8, NR))
    s_plane[y * X + x, :, NR:128] = jnp.zeros((8, 128 - NR), f32)
    for copy in stage_plane:
        copy.start()
    take(1, 2)
    send(1, 2)
    take(0, 3)
    finish(0)

    wait_for(s_plane.at[pl.ds(0, SIXTEEN - 1)], s_recv.at[0])
    s_line[core * Z + z] = jnp.sum(s_plane[...], axis=0)
    for copy in stage_line:
        copy.start()

    take(1, 3)
    finish(1)

    lam = scaled_loadings(load_v[14, 1], stress_col, first_ref[path], rows)
    lh, ll = split(lam)
    cov = (dot_nt(lh, lh) + dot_nt(lh, ll) + dot_nt(ll, lh)) * (LN2 * LN2)
    r0 = start_ref[pl.ds(path, 1), :]

    wait_for(z_buf, z_recv)
    bar, total = unpack(out_buf[14, 1] + jnp.sum(z_buf[...], axis=0))
    out[0:NR, 0:NR] = stress_col * bar
    through = jnp.sum(jnp.where(rows >= cols, cov, 0.0) * total, axis=0, keepdims=True)
    direct = jnp.sum(jnp.where(eye, total, 0.0), axis=0, keepdims=True)
    out[80:81, 0:NR] = direct / r0 + through * (100.0 / ((100.0 + r0) * (100.0 + r0)))

    results = [
        pltpu.make_async_copy(out.at[part], out_hbm.at[part], out_sem.at[i])
        for i, part in enumerate((pl.ds(0, 88), pl.ds(88, 8)))
    ]
    results[0].start()

    wait_for(out_buf.at[pl.ds(0, 12)], ring_send)
    wait_for(z_buf, z_send)
    for stage in range(2):
        wait_for(s_line.at[pl.ds(0, SIXTEEN - 1)], s_send.at[stage])
    wait_for(s_line.at[pl.ds(0, SIXTEEN - 1)], s_recv.at[1])
    out[88:96] = jnp.sum(s_line[...], axis=0)
    results[1].start()

    for copy in results:
        copy.wait()


def hand_on(packed, rate_out, vol_out, stress_out):
    rate_out[...] = packed[80:81, 0:NR]
    vol_out[0] = packed[0:NR, 0:NR]
    stress_out[...] = packed[88:89, 0:NR]


def body(start_rates, loadings, stress, increments, cotangent, first_active):
    log_paths = math.log2(WIDTH * X * Z)
    vmem = pl.BlockSpec(memory_space=pltpu.VMEM)
    anywhere = pl.BlockSpec(memory_space=pl.ANY)
    dma = pltpu.SemaphoreType.DMA
    summed = pl.pallas_call(
        lambda *refs: kernel(log_paths, *refs),
        out_shape=jax.ShapeDtypeStruct((96, 128), f32),
        in_specs=[anywhere] * 6,
        out_specs=anywhere,
        scratch_shapes=[
            pltpu.VMEM((1, NR), f32),
            pltpu.SMEM((2 * PAIRS,), jnp.int32),
            pltpu.VMEM((2 * PAIRS, NR), f32),
            pltpu.VMEM((96, 128), f32),
            pltpu.VMEM((PAIRS, 2, NR, NR), f32),
            pltpu.VMEM((PAIRS, 2, 2, NR, WIDTH), bf16),
            pltpu.VMEM((PAIRS, 2, NR, WIDTH), f32),
            pltpu.VMEM((PAIRS, 2, PACKED, 128), f32),
            pltpu.VMEM((2, 3, 2, 2, PACKED, 128), f32),
            pltpu.VMEM((Z - 1, PACKED, 128), f32),
            pltpu.VMEM((NR, NR), f32),
            pltpu.VMEM((SIXTEEN, 8, 128), f32),
            pltpu.VMEM((SIXTEEN, 8, 128), f32),
            pltpu.VMEM((2, 8, NR, NR), f32),
            pltpu.VMEM((2, 8, NR, NR), bf16),
            pltpu.VMEM((2, 8, NR, WIDTH), bf16),
            pltpu.VMEM((2, 8, NR, WIDTH), f32),
            pltpu.VMEM((2, 8, NR, WIDTH), f32),
            dma((3,)),
            dma((2,)),
            dma((3, 4)),
            dma(()),
            dma((2, 3)),
            dma(()),
            dma(()),
            dma((2,)),
            dma((2,)),
        ],
        compiler_params=pltpu.CompilerParams(
            collective_id=0, has_side_effects=True, vmem_limit_bytes=56 * 2**20
        ),
        name="adjoint",
    )(
        stress[None],
        first_active,
        start_rates,
        loadings.reshape(X, Z, NR, NR),
        increments.reshape(X, Z, 2, NR, WIDTH),
        cotangent.reshape(X, Z, NR, WIDTH),
    )
    rate, vol, stress_gradient = pl.pallas_call(
        hand_on,
        out_shape=(
            jax.ShapeDtypeStruct((1, NR), f32),
            jax.ShapeDtypeStruct((1, NR, NR), f32),
            jax.ShapeDtypeStruct((1, NR), f32),
        ),
        in_specs=[vmem],
        out_specs=(vmem, vmem, vmem),
        name="results",
    )(summed)
    return rate, vol, stress_gradient[0]


def solution(mesh):
    return jax.shard_map(
        body,
        mesh=mesh,
        in_specs=(
            P("grp", None),
            P("grp", None, None),
            P(),
            P("grp", None, None, "path"),
            P("grp", None, "path"),
            P("grp"),
        ),
        out_specs=(P(("grp", "path"), None), P(("grp", "path"), None, None), P()),
        check_vma=False,
    )
```

```python
import math

import jax
import jax.numpy as jnp
from jax import lax
from jax.experimental import pallas as pl
from jax.experimental.pallas import tpu as pltpu
from jax.sharding import PartitionSpec as P

NR = 80
WIDTH = 256
X, Z = 4, 8
Y, CORES = 4, 2
SIXTEEN = X * Y
PAIRS = 16
PACKED = 56
LN2 = math.log(2.0)
LOG2E = 1.0 / LN2
bf16 = jnp.bfloat16
f32 = jnp.float32
MESH = pl.DeviceIdType.MESH


def dot(a, b):
    return jnp.dot(a, b, preferred_element_type=f32)


def dot_nt(a, b):
    return lax.dot_general(a, b, (((1,), (1,)), ((), ())), preferred_element_type=f32)


def split(value):
    high = value.astype(bf16)
    return high, (value - high.astype(f32)).astype(bf16)


def index_masks():
    rows = lax.broadcasted_iota(jnp.int32, (NR, NR), 0)
    cols = lax.broadcasted_iota(jnp.int32, (NR, NR), 1)
    return rows, cols


STEPS = {(0, 0): 0, (0, 1): 1, (1, 0): 2, (0, 2): 3, (1, 1): 4, (0, 3): 5, (1, 2): 6, (1, 3): 7}


def place(pair, k, x):
    at, way = pair // 2, pair % 2
    half = (at + 1) % 2 - (7 - at) // 7 + at // 7
    step = (at + 1 - 2 * half) // 2
    reach = 2 - (step + 1) // 2
    side = lax.rem(step + way, 2)
    hops = 3 - 2 * half - side if k else 4 + 2 * half + side
    return lax.rem(x + reach * (1 - way) + (X - reach) * way, X), hops


def scaled_loadings(load, stress_col, first, rows):
    return load * jnp.where(rows >= first, stress_col * LOG2E, 0.0)


def forward(items, held, slot, masks, stress_col, log_paths):
    rows, cols = index_masks()
    eye = rows == cols
    for k, d in enumerate(items):
        yield
        d["lam"] = scaled_loadings(d["load"][...], stress_col, d["first"], rows)
        d["lh"], d["ll"] = split(d["lam"])
        held["lam"][slot, k] = d["lam"]
    for d in items:
        yield
        d["cov"] = dot_nt(d["lh"], d["lh"])
    for k, d in enumerate(items):
        yield
        drift = d["cov"] * masks[0]
        r0 = d["r0"]
        accrual = r0 / (100.0 + r0)
        half = jnp.sum(d["lam"] * d["lam"], axis=1, keepdims=True) * (-0.5 * LN2)
        c1 = jnp.sum(drift * accrual + jnp.where(eye, jnp.log2(r0), 0.0), axis=1, keepdims=True)
        d["c1"] = half + c1 - math.log2(100.0)
        d["c2"] = half + (math.log2(100.0) - log_paths)
        d["left"] = jnp.concatenate([d["lh"], d["ll"], drift.astype(bf16)], axis=1)
        held["back"][slot, k] = (d["cov"] * masks[1]).astype(bf16)
    for d in items:
        yield
        z1 = d["z"][0]
        d["e1"] = dot(d["left"][:, : 2 * NR], jnp.concatenate([z1, z1], axis=0))
    for k, d in enumerate(items):
        yield
        mid = jnp.exp2(d["e1"] + d["c1"])
        inverse = 1.0 / (1.0 + mid)
        accrual = mid * inverse
        d["mid"], d["a"] = mid, accrual.astype(bf16)
        held["a"][slot, k] = d["a"]
        held["slope"][slot, k] = accrual * inverse
    for d in items:
        yield
        z2 = d["z"][1]
        d["e2"] = dot(d["left"], jnp.concatenate([z2, z2, d["a"]], axis=0))
    for k, d in enumerate(items):
        yield
        held["g2"][slot, k] = d["mid"] * jnp.exp2(d["e2"] + d["c2"]) * d["cot"][...]


def adjoint(items, held, slot, emit):
    rows, cols = index_masks()
    low = rows >= cols
    ones = jnp.ones((16, WIDTH), bf16)
    gap = jnp.zeros((32, WIDTH), bf16)
    for k, d in enumerate(items):
        yield
        d["g2"] = held["g2"][slot, k]
        d["g2h"], d["g2l"] = split(d["g2"])
    for k, d in enumerate(items):
        yield
        d["da"] = dot(held["back"][slot, k], d["g2h"])
    for k, d in enumerate(items):
        yield
        right = jnp.concatenate([d["z"][1], ones, gap, held["a"][slot, k]], axis=0)
        d["sums2"] = dot_nt(jnp.concatenate([d["g2h"], d["g2l"]], axis=0), right)
    for k, d in enumerate(items):
        yield
        g1h, g1l = split(d["g2"] + held["slope"][slot, k] * d["da"])
        right = jnp.concatenate([d["z"][0], ones], axis=0)
        d["sums1"] = dot_nt(jnp.concatenate([g1h, g1l], axis=0), right)
    for k, d in enumerate(items):
        yield
        lam = held["lam"][slot, k]
        lh, ll = split(lam)
        sum1 = d["sums1"][:NR] + d["sums1"][NR:]
        sum2 = d["sums2"][:NR, :128] + d["sums2"][NR:, :128]
        outer = d["sums2"][:NR, 128:208] + d["sums2"][NR:, 128:208]
        total1, total2 = sum1[:, NR : NR + 1], sum2[:, NR : NR + 1]
        bar_cov = jnp.where(low, outer + total1 * (d["r0"] / (100.0 + d["r0"])), 0.0)
        mh, ml = split((bar_cov + bar_cov.T) * LN2)
        both = dot(jnp.concatenate([mh, ml], axis=0), lh)
        through = both[:NR] + both[NR:] + dot(mh, ll)
        bar = sum1[:, :NR] + sum2[:, :NR] + through - ((total1 + total2) * LN2) * lam
        emit(d, jnp.where(rows >= d["first"], bar, 0.0), total1)


def interleaved(*parts):
    parts = list(parts)
    while parts:
        for part in list(parts):
            if next(part, parts) is parts:
                parts.remove(part)


def wait_for(ref, sem):
    pltpu.make_async_copy(ref, ref, sem).wait()


def pack(ref, bar, total):
    ref[:, 0:NR] = bar[:PACKED]
    ref[:, NR : NR + 1] = total[:PACKED]
    rest = jnp.concatenate([bar[PACKED:], total[PACKED:]], axis=1)
    ref[0:24, 81:128] = rest[:, 0:47]
    ref[24:48, 81:115] = rest[:, 47:81]
    ref[24:48, 115:128] = jnp.zeros((24, 13), f32)
    ref[48:56, 81:128] = jnp.zeros((8, 47), f32)


def unpack(value):
    rest = jnp.concatenate([value[0:24, 81:128], value[24:48, 81:115]], axis=1)
    bar = jnp.concatenate([value[:, 0:NR], rest[:, 0:NR]], axis=0)
    total = jnp.concatenate([value[:, NR : NR + 1], rest[:, NR : NR + 1]], axis=0)
    return bar, total


def kernel(
    log_paths,
    stress_hbm, first_hbm, start_hbm, load_hbm, z_hbm, cot_hbm,
    out_hbm,
    stress_ref, first_ref, start_ref, out,
    load_v, z_v, cot_v, out_buf, ring_buf, z_buf, acc, s_plane, s_line,
    h_lam, h_back, h_a, h_slope, h_g2,
    small_sem, out_sem, in_sem, ring_send, ring_recv, z_send, z_recv, s_send, s_recv,
):
    g = lax.axis_index("grp")
    path = lax.axis_index("path")
    x, z = path // Z, lax.rem(path, Z)

    def owner(pair, k):
        owner_x, hops = place(pair, k, x)
        return owner_x, lax.rem(z + hops, Z)

    def fetches(pair):
        return [
            pltpu.make_async_copy(hbm.at[owner(pair, k)], vmem.at[pair, k], in_sem.at[i, pair // 4])
            for k in range(2)
            for i, (hbm, vmem) in enumerate(((load_hbm, load_v), (z_hbm, z_v), (cot_hbm, cot_v)))
        ]

    small = [
        pltpu.make_async_copy(hbm, here, small_sem.at[i])
        for i, (hbm, here) in enumerate(((stress_hbm, stress_ref), (first_hbm, first_ref), (start_hbm, start_ref)))
    ]
    for copy in small:
        copy.start()

    @pl.loop(0, 4)
    def _(pair):
        for copy in fetches(pair):
            copy.start()

    def x_peer(k):
        return (g, lax.rem(x + k, X) * Z + z)

    def z_peer(k):
        return (g, x * Z + lax.rem(z + k, Z))

    y, core = g // CORES, lax.rem(g, CORES)

    def plane_peer(k):
        return (lax.rem(y + k // X, Y) * CORES + core, lax.rem(x + k % X, X) * Z + z)

    def line_peer(k):
        return (y * CORES + lax.rem(core + k // Z, CORES), x * Z + lax.rem(z + k % Z, Z))

    barrier = pltpu.get_barrier_semaphore()
    for k in range(1, SIXTEEN):
        for peer in (plane_peer, line_peer):
            pl.semaphore_signal(barrier, inc=1, device_id=peer(k), device_id_type=MESH)

    @pl.loop(4, PAIRS)
    def _(pair):
        for copy in fetches(pair):
            copy.start()

    for copy in small:
        copy.wait()
    rows, cols = index_masks()
    eye = rows == cols
    stress_col = jnp.sum(jnp.where(eye, stress_ref[...], 0.0), axis=1, keepdims=True)
    acc[...] = jnp.zeros_like(acc)

    def ring(way, half, step):
        return pltpu.make_async_remote_copy(
            src_ref=out_buf.at[2 * STEPS[half, step] + way],
            dst_ref=ring_buf.at[half, step, way],
            send_sem=ring_send,
            recv_sem=ring_recv.at[half, step],
            device_id=x_peer(X - 1 if way else 1),
            device_id_type=MESH,
        )

    def hand_over(half, side, k):
        hops = 3 - 2 * half - side if k else 4 + 2 * half + side
        return pltpu.make_async_remote_copy(
            src_ref=out_buf.at[2 * STEPS[half, 3] + 1 - side, k],
            dst_ref=z_buf.at[hops - 1],
            send_sem=z_send,
            recv_sem=z_recv,
            device_id=z_peer(hops),
            device_id_type=MESH,
        )

    handed = [(0, side, k) for side in range(2) for k in range(2)], [(1, 0, 0), (1, 0, 1), (1, 1, 0)]

    def arrived(half, step):
        wait_for(ring_buf.at[half, step], ring_recv.at[half, step])

    def finish(half):
        arrived(half, 2)
        for way in range(2):
            out_buf[2 * STEPS[half, 3] + 1 - way] += ring_buf[half, 2, way]
        for what in handed[half]:
            hand_over(*what).start()

    def emit(d, bar, total):
        pack(d["out"], bar, total)
        acc[...] += d["load"][...] * bar

    def scenario(pair, k):
        owner_x, owner_z = owner(pair, k)
        s = owner_x * Z + owner_z
        return dict(
            load=load_v.at[pair, k], z=z_v.at[pair, k], cot=cot_v.at[pair, k], out=out_buf.at[pair, k],
            first=first_ref[s], r0=start_ref[pl.ds(s, 1), :],
        )

    def share(buf, peer, me, stage):
        return [
            pltpu.make_async_remote_copy(
                src_ref=buf.at[me],
                dst_ref=buf.at[me],
                send_sem=s_send.at[stage],
                recv_sem=s_recv.at[stage],
                device_id=peer(k),
                device_id_type=MESH,
            )
            for k in range(1, SIXTEEN)
        ]

    stage_plane = share(s_plane, plane_peer, y * X + x, 0)
    stage_line = share(s_line, line_peer, core * Z + z, 1)

    masks = (jnp.where(rows >= cols, LN2, 0.0), jnp.where(rows <= cols, LN2 * LN2, 0.0))
    held = dict(lam=h_lam, back=h_back, a=h_a, slope=h_slope, g2=h_g2)

    def items(group):
        return [scenario(4 * group + j, k) for j in range(4) for k in range(2)]

    def start(group, slot):
        blocks = pl.ds(4 * group, 4)
        for i, vmem in enumerate((load_v, z_v, cot_v)):
            wait_for(vmem.at[blocks], in_sem.at[i, group])
        return forward(items(group), held, slot, masks, stress_col, log_paths)

    def send(half, step):
        for way in range(2):
            ring(way, half, step).start()

    def take(half, step):
        arrived(half, step - 2)
        for way in range(2):
            out_buf[2 * STEPS[half, step] + way] += ring_buf[half, step - 2, way]

    interleaved(start(0, 0))

    @pl.loop(1, 4)
    def _(group):
        slot = lax.rem(group, 2)
        ahead = start(group, slot)
        interleaved(adjoint(items(group - 1), held, 1 - slot, emit), ahead)

        @pl.when(group == 1)
        def _():
            pl.semaphore_wait(barrier, 2 * (SIXTEEN - 1))
            send(0, 0)
            send(0, 1)

        @pl.when(group == 2)
        def _():
            send(1, 0)

        @pl.when(group == 3)
        def _():
            take(0, 2)
            send(0, 2)
            send(1, 1)

    interleaved(adjoint(items(3), held, 1, emit))
    part = jnp.sum(jnp.where(eye, jnp.sum(acc[...], axis=1, keepdims=True), 0.0), axis=0, keepdims=True)
    s_plane[y * X + x] = jnp.concatenate([part, jnp.zeros((1, 128 - NR), f32)], axis=1)
    for copy in stage_plane:
        copy.start()
    take(1, 2)
    send(1, 2)
    take(0, 3)
    finish(0)

    wait_for(s_plane.at[pl.ds(0, SIXTEEN - 1)], s_recv.at[0])
    s_line[core * Z + z] = jnp.sum(s_plane[...], axis=0)
    for copy in stage_line:
        copy.start()

    take(1, 3)
    finish(1)

    lam = scaled_loadings(load_v[14, 1], stress_col, first_ref[path], rows)
    lh, ll = split(lam)
    cov = (dot_nt(lh, lh) + dot_nt(lh, ll) + dot_nt(ll, lh)) * (LN2 * LN2)
    r0 = start_ref[pl.ds(path, 1), :]

    wait_for(z_buf, z_recv)
    bar, total = unpack(out_buf[14, 1] + jnp.sum(z_buf[...], axis=0))
    out[0:NR, 0:NR] = stress_col * bar
    through = jnp.sum(jnp.where(rows >= cols, cov, 0.0) * total, axis=0, keepdims=True)
    direct = jnp.sum(jnp.where(eye, total, 0.0), axis=0, keepdims=True)
    out[80:81, 0:NR] = direct / r0 + through * (100.0 / ((100.0 + r0) * (100.0 + r0)))

    results = [
        pltpu.make_async_copy(out.at[part], out_hbm.at[part], out_sem.at[i])
        for i, part in enumerate((pl.ds(0, 88), pl.ds(88, 8)))
    ]
    results[0].start()

    wait_for(out_buf.at[pl.ds(0, 12)], ring_send)
    wait_for(z_buf, z_send)
    for stage in range(2):
        wait_for(s_line.at[pl.ds(0, SIXTEEN - 1)], s_send.at[stage])
    wait_for(s_line.at[pl.ds(0, SIXTEEN - 1)], s_recv.at[1])
    out[88:89] = jnp.sum(s_line[...], axis=0)
    results[1].start()

    for copy in results:
        copy.wait()


def hand_on(packed, rate_out, vol_out, stress_out):
    rate_out[...] = packed[80:81, 0:NR]
    vol_out[0] = packed[0:NR, 0:NR]
    stress_out[...] = packed[88:89, 0:NR]


def body(start_rates, loadings, stress, increments, cotangent, first_active):
    log_paths = math.log2(WIDTH * X * Z)
    vmem = pl.BlockSpec(memory_space=pltpu.VMEM)
    anywhere = pl.BlockSpec(memory_space=pl.ANY)
    dma = pltpu.SemaphoreType.DMA
    summed = pl.pallas_call(
        lambda *refs: kernel(log_paths, *refs),
        out_shape=jax.ShapeDtypeStruct((96, 128), f32),
        in_specs=[anywhere] * 6,
        out_specs=anywhere,
        scratch_shapes=[
            pltpu.VMEM((1, NR), f32),
            pltpu.SMEM((2 * PAIRS,), jnp.int32),
            pltpu.VMEM((2 * PAIRS, NR), f32),
            pltpu.VMEM((96, 128), f32),
            pltpu.VMEM((PAIRS, 2, NR, NR), f32),
            pltpu.VMEM((PAIRS, 2, 2, NR, WIDTH), bf16),
            pltpu.VMEM((PAIRS, 2, NR, WIDTH), f32),
            pltpu.VMEM((PAIRS, 2, PACKED, 128), f32),
            pltpu.VMEM((2, 3, 2, 2, PACKED, 128), f32),
            pltpu.VMEM((Z - 1, PACKED, 128), f32),
            pltpu.VMEM((NR, NR), f32),
            pltpu.VMEM((SIXTEEN, 1, 128), f32),
            pltpu.VMEM((SIXTEEN, 1, 128), f32),
            pltpu.VMEM((2, 8, NR, NR), f32),
            pltpu.VMEM((2, 8, NR, NR), bf16),
            pltpu.VMEM((2, 8, NR, WIDTH), bf16),
            pltpu.VMEM((2, 8, NR, WIDTH), f32),
            pltpu.VMEM((2, 8, NR, WIDTH), f32),
            dma((3,)),
            dma((2,)),
            dma((3, 4)),
            dma(()),
            dma((2, 3)),
            dma(()),
            dma(()),
            dma((2,)),
            dma((2,)),
        ],
        compiler_params=pltpu.CompilerParams(
            collective_id=0, has_side_effects=True, vmem_limit_bytes=56 * 2**20
        ),
        name="adjoint",
    )(
        stress[None],
        first_active,
        start_rates,
        loadings.reshape(X, Z, NR, NR),
        increments.reshape(X, Z, 2, NR, WIDTH),
        cotangent.reshape(X, Z, NR, WIDTH),
    )
    rate, vol, stress_gradient = pl.pallas_call(
        hand_on,
        out_shape=(
            jax.ShapeDtypeStruct((1, NR), f32),
            jax.ShapeDtypeStruct((1, NR, NR), f32),
            jax.ShapeDtypeStruct((1, NR), f32),
        ),
        in_specs=[vmem],
        out_specs=(vmem, vmem, vmem),
        name="results",
    )(summed)
    return rate, vol, stress_gradient[0]


def solution(mesh):
    return jax.shard_map(
        body,
        mesh=mesh,
        in_specs=(
            P("grp", None),
            P("grp", None, None),
            P(),
            P("grp", None, None, "path"),
            P("grp", None, "path"),
            P("grp"),
        ),
        out_specs=(P(("grp", "path"), None), P(("grp", "path"), None, None), P()),
        check_vma=False,
    )
```

```python
import math

import jax
import jax.numpy as jnp
from jax import lax
from jax.experimental import pallas as pl
from jax.experimental.pallas import tpu as pltpu
from jax.sharding import PartitionSpec as P

NR = 80
WIDTH = 256
X, Z = 4, 8
Y, CORES = 4, 2
SIXTEEN = X * Y
PAIRS = 16
PACKED = 56
LN2 = math.log(2.0)
LOG2E = 1.0 / LN2
bf16 = jnp.bfloat16
f32 = jnp.float32
MESH = pl.DeviceIdType.MESH


def dot(a, b):
    return jnp.dot(a, b, preferred_element_type=f32)


def dot_nt(a, b):
    return lax.dot_general(a, b, (((1,), (1,)), ((), ())), preferred_element_type=f32)


def split(value):
    high = value.astype(bf16)
    return high, (value - high.astype(f32)).astype(bf16)


def index_masks():
    rows = lax.broadcasted_iota(jnp.int32, (NR, NR), 0)
    cols = lax.broadcasted_iota(jnp.int32, (NR, NR), 1)
    return rows, cols


STEPS = {(0, 0): 0, (0, 1): 1, (1, 0): 2, (0, 2): 3, (1, 1): 4, (0, 3): 5, (1, 2): 6, (1, 3): 7}


def place(pair, k, x):
    at, way = pair // 2, pair % 2
    half = (at + 1) % 2 - (7 - at) // 7 + at // 7
    step = (at + 1 - 2 * half) // 2
    reach = 2 - (step + 1) // 2
    side = lax.rem(step + way, 2)
    hops = 3 - 2 * half - side if k else 4 + 2 * half + side
    return lax.rem(x + reach * (1 - way) + (X - reach) * way, X), hops


def scaled_loadings(load, stress_col, first, rows):
    return load * jnp.where(rows >= first, stress_col * LOG2E, 0.0)


def forward(items, held, slot, masks, stress_col, log_paths):
    rows, cols = index_masks()
    eye = rows == cols
    pad = jnp.zeros((NR, 128 - NR), bf16)
    gap = jnp.zeros((128 - NR, WIDTH), bf16)
    for k, d in enumerate(items):
        yield
        d["lam"] = scaled_loadings(d["load"][...], stress_col, d["first"], rows)
        d["lh"], d["ll"] = split(d["lam"])
        held["lam"][slot, k] = d["lam"]
    for d in items:
        yield
        d["cov"] = dot_nt(d["lh"], d["lh"])
    for k, d in enumerate(items):
        yield
        drift = d["cov"] * masks[0]
        r0 = d["r0"]
        accrual = r0 / (100.0 + r0)
        half = jnp.sum(d["lam"] * d["lam"], axis=1, keepdims=True) * (-0.5 * LN2)
        c1 = jnp.sum(drift * accrual + jnp.where(eye, jnp.log2(r0), 0.0), axis=1, keepdims=True)
        d["c1"] = half + c1 - math.log2(100.0)
        d["c2"] = half + (math.log2(100.0) - log_paths)
        d["left"] = jnp.concatenate([d["lh"], pad, d["ll"]], axis=1)
        d["drift"] = drift.astype(bf16)
        held["back"][slot, k] = (d["cov"] * masks[1]).astype(bf16)
    for d in items:
        yield
        z1 = d["z"][0]
        d["e1"] = dot(d["left"], jnp.concatenate([z1, gap, z1], axis=0))
    for k, d in enumerate(items):
        yield
        mid = jnp.exp2(d["e1"] + d["c1"])
        inverse = 1.0 / (1.0 + mid)
        accrual = mid * inverse
        d["mid"], d["a"] = mid, accrual.astype(bf16)
        held["a"][slot, k] = d["a"]
        held["slope"][slot, k] = accrual * inverse
    for d in items:
        yield
        z2 = d["z"][1]
        d["e2"] = dot(d["left"], jnp.concatenate([z2, gap, z2], axis=0)) + dot(d["drift"], d["a"])
    for k, d in enumerate(items):
        yield
        held["g2"][slot, k] = d["mid"] * jnp.exp2(d["e2"] + d["c2"]) * d["cot"][...]


def adjoint(items, held, slot, emit):
    rows, cols = index_masks()
    low = rows >= cols
    ones = jnp.ones((16, WIDTH), bf16)
    many = jnp.ones((128, WIDTH), bf16)
    gap = jnp.zeros((32, WIDTH), bf16)
    for k, d in enumerate(items):
        yield
        d["g2"] = held["g2"][slot, k]
        d["g2h"], d["g2l"] = split(d["g2"])
    for k, d in enumerate(items):
        yield
        d["da"] = dot(held["back"][slot, k], d["g2h"])
    for k, d in enumerate(items):
        yield
        right = jnp.concatenate([d["z"][1], ones, gap, held["a"][slot, k]], axis=0)
        d["sums2"] = dot_nt(jnp.concatenate([d["g2h"], d["g2l"]], axis=0), right)
    for k, d in enumerate(items):
        yield
        g1h, g1l = split(d["g2"] + held["slope"][slot, k] * d["da"])
        right = jnp.concatenate([d["z"][0], many], axis=0)
        d["sums1"] = dot_nt(jnp.concatenate([g1h, g1l], axis=0), right)
    for k, d in enumerate(items):
        yield
        lam = held["lam"][slot, k]
        lh, ll = split(lam)
        sum1 = d["sums1"][:NR, :128] + d["sums1"][NR:, :128]
        whole1 = d["sums1"][:NR, 128:208] + d["sums1"][NR:, 128:208]
        sum2 = d["sums2"][:NR, :128] + d["sums2"][NR:, :128]
        outer = d["sums2"][:NR, 128:208] + d["sums2"][NR:, 128:208]
        total1, total2 = sum1[:, NR : NR + 1], sum2[:, NR : NR + 1]
        bar_cov = jnp.where(low, outer + whole1 * (d["r0"] / (100.0 + d["r0"])), 0.0)
        mh, ml = split((bar_cov + bar_cov.T) * LN2)
        both = dot(jnp.concatenate([mh, ml], axis=0), lh)
        through = both[:NR] + both[NR:] + dot(mh, ll)
        bar = sum1[:, :NR] + sum2[:, :NR] + through - ((whole1 + total2) * LN2) * lam
        emit(d, jnp.where(rows >= d["first"], bar, 0.0), total1)


def interleaved(*parts):
    parts = list(parts)
    while parts:
        for part in list(parts):
            if next(part, parts) is parts:
                parts.remove(part)


def wait_for(ref, sem):
    pltpu.make_async_copy(ref, ref, sem).wait()


def pack(ref, bar, total):
    ref[:, 0:NR] = bar[:PACKED]
    ref[:, NR : NR + 1] = total[:PACKED]
    rest = jnp.concatenate([bar[PACKED:], total[PACKED:]], axis=1)
    ref[0:24, 81:128] = rest[:, 0:47]
    ref[24:48, 81:115] = rest[:, 47:81]
    ref[24:48, 115:128] = jnp.zeros((24, 13), f32)
    ref[48:56, 81:128] = jnp.zeros((8, 47), f32)


def unpack(value):
    rest = jnp.concatenate([value[0:24, 81:128], value[24:48, 81:115]], axis=1)
    bar = jnp.concatenate([value[:, 0:NR], rest[:, 0:NR]], axis=0)
    total = jnp.concatenate([value[:, NR : NR + 1], rest[:, NR : NR + 1]], axis=0)
    return bar, total


def kernel(
    log_paths,
    stress_hbm, first_hbm, start_hbm, load_hbm, z_hbm, cot_hbm,
    out_hbm,
    stress_ref, first_ref, start_ref, out,
    load_v, z_v, cot_v, out_buf, ring_buf, z_buf, acc, s_plane, s_line,
    h_lam, h_back, h_a, h_slope, h_g2,
    small_sem, out_sem, in_sem, ring_send, ring_recv, z_send, z_recv, s_send, s_recv,
):
    g = lax.axis_index("grp")
    path = lax.axis_index("path")
    x, z = path // Z, lax.rem(path, Z)

    def owner(pair, k):
        owner_x, hops = place(pair, k, x)
        return owner_x, lax.rem(z + hops, Z)

    def fetches(pair):
        return [
            pltpu.make_async_copy(hbm.at[owner(pair, k)], vmem.at[pair, k], in_sem.at[i, pair // 4])
            for k in range(2)
            for i, (hbm, vmem) in enumerate(((load_hbm, load_v), (z_hbm, z_v), (cot_hbm, cot_v)))
        ]

    small = [
        pltpu.make_async_copy(hbm, here, small_sem.at[i])
        for i, (hbm, here) in enumerate(((stress_hbm, stress_ref), (first_hbm, first_ref), (start_hbm, start_ref)))
    ]
    for copy in small:
        copy.start()

    @pl.loop(0, 4)
    def _(pair):
        for copy in fetches(pair):
            copy.start()

    def x_peer(k):
        return (g, lax.rem(x + k, X) * Z + z)

    def z_peer(k):
        return (g, x * Z + lax.rem(z + k, Z))

    y, core = g // CORES, lax.rem(g, CORES)

    def plane_peer(k):
        return (lax.rem(y + k // X, Y) * CORES + core, lax.rem(x + k % X, X) * Z + z)

    def line_peer(k):
        return (y * CORES + lax.rem(core + k // Z, CORES), x * Z + lax.rem(z + k % Z, Z))

    barrier = pltpu.get_barrier_semaphore()
    for k in range(1, SIXTEEN):
        for peer in (plane_peer, line_peer):
            pl.semaphore_signal(barrier, inc=1, device_id=peer(k), device_id_type=MESH)

    @pl.loop(4, PAIRS)
    def _(pair):
        for copy in fetches(pair):
            copy.start()

    for copy in small:
        copy.wait()
    rows, cols = index_masks()
    eye = rows == cols
    stress_col = jnp.sum(jnp.where(eye, stress_ref[...], 0.0), axis=1, keepdims=True)
    acc[...] = jnp.zeros_like(acc)

    def ring(way, half, step):
        return pltpu.make_async_remote_copy(
            src_ref=out_buf.at[2 * STEPS[half, step] + way],
            dst_ref=ring_buf.at[half, step, way],
            send_sem=ring_send,
            recv_sem=ring_recv.at[half, step],
            device_id=x_peer(X - 1 if way else 1),
            device_id_type=MESH,
        )

    def hand_over(half, side, k):
        hops = 3 - 2 * half - side if k else 4 + 2 * half + side
        return pltpu.make_async_remote_copy(
            src_ref=out_buf.at[2 * STEPS[half, 3] + 1 - side, k],
            dst_ref=z_buf.at[hops - 1],
            send_sem=z_send,
            recv_sem=z_recv,
            device_id=z_peer(hops),
            device_id_type=MESH,
        )

    handed = [(0, side, k) for side in range(2) for k in range(2)], [(1, 0, 0), (1, 0, 1), (1, 1, 0)]

    def arrived(half, step):
        wait_for(ring_buf.at[half, step], ring_recv.at[half, step])

    def finish(half):
        arrived(half, 2)
        for way in range(2):
            out_buf[2 * STEPS[half, 3] + 1 - way] += ring_buf[half, 2, way]
        for what in handed[half]:
            hand_over(*what).start()

    def emit(d, bar, total):
        pack(d["out"], bar, total)
        acc[...] += d["load"][...] * bar

    def scenario(pair, k):
        owner_x, owner_z = owner(pair, k)
        s = owner_x * Z + owner_z
        return dict(
            load=load_v.at[pair, k], z=z_v.at[pair, k], cot=cot_v.at[pair, k], out=out_buf.at[pair, k],
            first=first_ref[s], r0=start_ref[pl.ds(s, 1), :],
        )

    def share(buf, peer, me, stage):
        return [
            pltpu.make_async_remote_copy(
                src_ref=buf.at[me],
                dst_ref=buf.at[me],
                send_sem=s_send.at[stage],
                recv_sem=s_recv.at[stage],
                device_id=peer(k),
                device_id_type=MESH,
            )
            for k in range(1, SIXTEEN)
        ]

    stage_plane = share(s_plane, plane_peer, y * X + x, 0)
    stage_line = share(s_line, line_peer, core * Z + z, 1)

    masks = (jnp.where(rows >= cols, LN2, 0.0), jnp.where(rows <= cols, LN2 * LN2, 0.0))
    held = dict(lam=h_lam, back=h_back, a=h_a, slope=h_slope, g2=h_g2)

    def items(group):
        return [scenario(4 * group + j, k) for j in range(4) for k in range(2)]

    def start(group, slot):
        blocks = pl.ds(4 * group, 4)
        for i, vmem in enumerate((load_v, z_v, cot_v)):
            wait_for(vmem.at[blocks], in_sem.at[i, group])
        return forward(items(group), held, slot, masks, stress_col, log_paths)

    def send(half, step):
        for way in range(2):
            ring(way, half, step).start()

    def take(half, step):
        arrived(half, step - 2)
        for way in range(2):
            out_buf[2 * STEPS[half, step] + way] += ring_buf[half, step - 2, way]

    interleaved(start(0, 0))

    @pl.loop(1, 4)
    def _(group):
        slot = lax.rem(group, 2)
        ahead = start(group, slot)
        interleaved(adjoint(items(group - 1), held, 1 - slot, emit), ahead)

        @pl.when(group == 1)
        def _():
            pl.semaphore_wait(barrier, 2 * (SIXTEEN - 1))
            send(0, 0)
            send(0, 1)

        @pl.when(group == 2)
        def _():
            send(1, 0)

        @pl.when(group == 3)
        def _():
            take(0, 2)
            send(0, 2)
            send(1, 1)

    interleaved(adjoint(items(3), held, 1, emit))
    part = jnp.sum(jnp.where(eye, jnp.sum(acc[...], axis=1, keepdims=True), 0.0), axis=0, keepdims=True)
    s_plane[y * X + x] = jnp.concatenate([part, jnp.zeros((1, 128 - NR), f32)], axis=1)
    for copy in stage_plane:
        copy.start()
    take(1, 2)
    send(1, 2)
    take(0, 3)
    finish(0)

    wait_for(s_plane.at[pl.ds(0, SIXTEEN - 1)], s_recv.at[0])
    s_line[core * Z + z] = jnp.sum(s_plane[...], axis=0)
    for copy in stage_line:
        copy.start()

    take(1, 3)
    finish(1)

    lam = scaled_loadings(load_v[14, 1], stress_col, first_ref[path], rows)
    lh, ll = split(lam)
    cov = (dot_nt(lh, lh) + dot_nt(lh, ll) + dot_nt(ll, lh)) * (LN2 * LN2)
    r0 = start_ref[pl.ds(path, 1), :]

    wait_for(z_buf, z_recv)
    bar, total = unpack(out_buf[14, 1] + jnp.sum(z_buf[...], axis=0))
    out[0:NR, 0:NR] = stress_col * bar
    through = jnp.sum(jnp.where(rows >= cols, cov, 0.0) * total, axis=0, keepdims=True)
    direct = jnp.sum(jnp.where(eye, total, 0.0), axis=0, keepdims=True)
    out[80:81, 0:NR] = direct / r0 + through * (100.0 / ((100.0 + r0) * (100.0 + r0)))

    results = [
        pltpu.make_async_copy(out.at[part], out_hbm.at[part], out_sem.at[i])
        for i, part in enumerate((pl.ds(0, 88), pl.ds(88, 8)))
    ]
    results[0].start()

    wait_for(out_buf.at[pl.ds(0, 12)], ring_send)
    wait_for(z_buf, z_send)
    for stage in range(2):
        wait_for(s_line.at[pl.ds(0, SIXTEEN - 1)], s_send.at[stage])
    wait_for(s_line.at[pl.ds(0, SIXTEEN - 1)], s_recv.at[1])
    out[88:89] = jnp.sum(s_line[...], axis=0)
    results[1].start()

    for copy in results:
        copy.wait()


def hand_on(packed, rate_out, vol_out, stress_out):
    rate_out[...] = packed[80:81, 0:NR]
    vol_out[0] = packed[0:NR, 0:NR]
    stress_out[...] = packed[88:89, 0:NR]


def body(start_rates, loadings, stress, increments, cotangent, first_active):
    log_paths = math.log2(WIDTH * X * Z)
    vmem = pl.BlockSpec(memory_space=pltpu.VMEM)
    anywhere = pl.BlockSpec(memory_space=pl.ANY)
    dma = pltpu.SemaphoreType.DMA
    summed = pl.pallas_call(
        lambda *refs: kernel(log_paths, *refs),
        out_shape=jax.ShapeDtypeStruct((96, 128), f32),
        in_specs=[anywhere] * 6,
        out_specs=anywhere,
        scratch_shapes=[
            pltpu.VMEM((1, NR), f32),
            pltpu.SMEM((2 * PAIRS,), jnp.int32),
            pltpu.VMEM((2 * PAIRS, NR), f32),
            pltpu.VMEM((96, 128), f32),
            pltpu.VMEM((PAIRS, 2, NR, NR), f32),
            pltpu.VMEM((PAIRS, 2, 2, NR, WIDTH), bf16),
            pltpu.VMEM((PAIRS, 2, NR, WIDTH), f32),
            pltpu.VMEM((PAIRS, 2, PACKED, 128), f32),
            pltpu.VMEM((2, 3, 2, 2, PACKED, 128), f32),
            pltpu.VMEM((Z - 1, PACKED, 128), f32),
            pltpu.VMEM((NR, NR), f32),
            pltpu.VMEM((SIXTEEN, 1, 128), f32),
            pltpu.VMEM((SIXTEEN, 1, 128), f32),
            pltpu.VMEM((2, 8, NR, NR), f32),
            pltpu.VMEM((2, 8, NR, NR), bf16),
            pltpu.VMEM((2, 8, NR, WIDTH), bf16),
            pltpu.VMEM((2, 8, NR, WIDTH), f32),
            pltpu.VMEM((2, 8, NR, WIDTH), f32),
            dma((3,)),
            dma((2,)),
            dma((3, 4)),
            dma(()),
            dma((2, 3)),
            dma(()),
            dma(()),
            dma((2,)),
            dma((2,)),
        ],
        compiler_params=pltpu.CompilerParams(
            collective_id=0, has_side_effects=True, vmem_limit_bytes=56 * 2**20
        ),
        name="adjoint",
    )(
        stress[None],
        first_active,
        start_rates,
        loadings.reshape(X, Z, NR, NR),
        increments.reshape(X, Z, 2, NR, WIDTH),
        cotangent.reshape(X, Z, NR, WIDTH),
    )
    rate, vol, stress_gradient = pl.pallas_call(
        hand_on,
        out_shape=(
            jax.ShapeDtypeStruct((1, NR), f32),
            jax.ShapeDtypeStruct((1, NR, NR), f32),
            jax.ShapeDtypeStruct((1, NR), f32),
        ),
        in_specs=[vmem],
        out_specs=(vmem, vmem, vmem),
        name="results",
    )(summed)
    return rate, vol, stress_gradient[0]


def solution(mesh):
    return jax.shard_map(
        body,
        mesh=mesh,
        in_specs=(
            P("grp", None),
            P("grp", None, None),
            P(),
            P("grp", None, None, "path"),
            P("grp", None, "path"),
            P("grp"),
        ),
        out_specs=(P(("grp", "path"), None), P(("grp", "path"), None, None), P()),
        check_vma=False,
    )
```

```python
import math

import jax
import jax.numpy as jnp
from jax import lax
from jax.experimental import pallas as pl
from jax.experimental.pallas import tpu as pltpu
from jax.sharding import PartitionSpec as P

NR = 80
WIDTH = 256
X, Z = 4, 8
Y, CORES = 4, 2
SIXTEEN = X * Y
PAIRS = 16
PACKED = 56
LN2 = math.log(2.0)
LOG2E = 1.0 / LN2
bf16 = jnp.bfloat16
f32 = jnp.float32
MESH = pl.DeviceIdType.MESH


def dot(a, b):
    return jnp.dot(a, b, preferred_element_type=f32)


def dot_nt(a, b):
    return lax.dot_general(a, b, (((1,), (1,)), ((), ())), preferred_element_type=f32)


def split(value):
    high = value.astype(bf16)
    return high, (value - high.astype(f32)).astype(bf16)


def index_masks():
    rows = lax.broadcasted_iota(jnp.int32, (NR, NR), 0)
    cols = lax.broadcasted_iota(jnp.int32, (NR, NR), 1)
    return rows, cols


STEPS = {(0, 0): 0, (0, 1): 1, (1, 0): 2, (0, 2): 3, (1, 1): 4, (0, 3): 5, (1, 2): 6, (1, 3): 7}


def place(pair, k, x):
    at, way = pair // 2, pair % 2
    half = (at + 1) % 2 - (7 - at) // 7 + at // 7
    step = (at + 1 - 2 * half) // 2
    reach = 2 - (step + 1) // 2
    side = lax.rem(step + way, 2)
    hops = 3 - 2 * half - side if k else 4 + 2 * half + side
    return lax.rem(x + reach * (1 - way) + (X - reach) * way, X), hops


def scaled_loadings(load, stress_col, first, rows):
    return load * jnp.where(rows >= first, stress_col * LOG2E, 0.0)


def forward(items, held, slot, masks, stress_col, log_paths):
    rows, cols = index_masks()
    eye = rows == cols
    pad = jnp.zeros((NR, 128 - NR), bf16)
    gap = jnp.zeros((128 - NR, WIDTH), bf16)
    for k, d in enumerate(items):
        yield
        d["lam"] = scaled_loadings(d["load"][...], stress_col, d["first"], rows)
        d["lh"], d["ll"] = split(d["lam"])
        held["lam"][slot, k] = d["lam"]
    for d in items:
        yield
        d["cov"] = dot_nt(d["lh"], d["lh"])
    for k, d in enumerate(items):
        yield
        drift = d["cov"] * masks[0]
        r0 = d["r0"]
        accrual = r0 / (100.0 + r0)
        half = jnp.sum(d["lam"] * d["lam"], axis=1, keepdims=True) * (-0.5 * LN2)
        c1 = jnp.sum(drift * accrual + jnp.where(eye, jnp.log2(r0), 0.0), axis=1, keepdims=True)
        d["c1"] = half + c1 - math.log2(100.0)
        d["c2"] = half + (math.log2(100.0) - log_paths)
        d["left"] = jnp.concatenate([d["lh"], pad, d["ll"]], axis=1)
        d["drift"] = drift.astype(bf16)
        held["back"][slot, k] = (d["cov"] * masks[1]).astype(bf16)
    for d in items:
        yield
        z1 = d["z"][0]
        d["e1"] = dot(d["left"], jnp.concatenate([z1, gap, z1], axis=0))
    for k, d in enumerate(items):
        yield
        mid = jnp.exp2(d["e1"] + d["c1"])
        inverse = 1.0 / (1.0 + mid)
        accrual = mid * inverse
        d["mid"], d["a"] = mid, accrual.astype(bf16)
        held["a"][slot, k] = d["a"]
        held["slope"][slot, k] = accrual * inverse
    for d in items:
        yield
        z2 = d["z"][1]
        d["e2"] = dot(d["left"], jnp.concatenate([z2, gap, z2], axis=0)) + dot(d["drift"], d["a"])
    for k, d in enumerate(items):
        yield
        held["g2"][slot, k] = d["mid"] * jnp.exp2(d["e2"] + d["c2"]) * d["cot"][...]


def adjoint(items, held, slot, emit):
    rows, cols = index_masks()
    low = rows >= cols
    ones = jnp.ones((16, WIDTH), bf16)
    many = jnp.ones((128, WIDTH), bf16)
    gap = jnp.zeros((32, WIDTH), bf16)
    for k, d in enumerate(items):
        yield
        d["g2"] = held["g2"][slot, k]
        d["g2h"], d["g2l"] = split(d["g2"])
    for k, d in enumerate(items):
        yield
        d["da"] = dot(held["back"][slot, k], d["g2h"])
    for k, d in enumerate(items):
        yield
        right = jnp.concatenate([d["z"][1], ones, gap, held["a"][slot, k]], axis=0)
        d["sums2"] = dot_nt(jnp.concatenate([d["g2h"], d["g2l"]], axis=0), right)
    for k, d in enumerate(items):
        yield
        g1h, g1l = split(d["g2"] + held["slope"][slot, k] * d["da"])
        right = jnp.concatenate([d["z"][0], many], axis=0)
        d["sums1"] = dot_nt(jnp.concatenate([g1h, g1l], axis=0), right)
    for k, d in enumerate(items):
        yield
        lam = held["lam"][slot, k]
        lh, ll = split(lam)
        sum1 = d["sums1"][:NR, :128] + d["sums1"][NR:, :128]
        whole1 = d["sums1"][:NR, 128:208] + d["sums1"][NR:, 128:208]
        sum2 = d["sums2"][:NR, :128] + d["sums2"][NR:, :128]
        outer = d["sums2"][:NR, 128:208] + d["sums2"][NR:, 128:208]
        total1, total2 = sum1[:, NR : NR + 1], sum2[:, NR : NR + 1]
        bar_cov = jnp.where(low, outer + whole1 * (d["r0"] / (100.0 + d["r0"])), 0.0)
        mh, ml = split((bar_cov + bar_cov.T) * LN2)
        both = dot(jnp.concatenate([mh, ml], axis=0), lh)
        through = both[:NR] + both[NR:] + dot(mh, ll)
        bar = sum1[:, :NR] + sum2[:, :NR] + through - ((whole1 + total2) * LN2) * lam
        emit(d, jnp.where(rows >= d["first"], bar, 0.0), total1)


def interleaved(*parts):
    parts = list(parts)
    while parts:
        for part in list(parts):
            if next(part, parts) is parts:
                parts.remove(part)


def wait_for(ref, sem):
    pltpu.make_async_copy(ref, ref, sem).wait()


def pack(ref, bar, total):
    ref[:, 0:NR] = bar[:PACKED]
    ref[:, NR : NR + 1] = total[:PACKED]
    rest = jnp.concatenate([bar[PACKED:], total[PACKED:]], axis=1)
    ref[0:24, 81:128] = rest[:, 0:47]
    ref[24:48, 81:115] = rest[:, 47:81]
    ref[24:48, 115:128] = jnp.zeros((24, 13), f32)
    ref[48:56, 81:128] = jnp.zeros((8, 47), f32)


def unpack(value):
    rest = jnp.concatenate([value[0:24, 81:128], value[24:48, 81:115]], axis=1)
    bar = jnp.concatenate([value[:, 0:NR], rest[:, 0:NR]], axis=0)
    total = jnp.concatenate([value[:, NR : NR + 1], rest[:, NR : NR + 1]], axis=0)
    return bar, total


def kernel(
    log_paths,
    stress_hbm, first_hbm, start_hbm, load_hbm, z_hbm, cot_hbm,
    out_hbm,
    stress_ref, first_ref, start_ref, out,
    load_v, z_v, cot_v, out_buf, ring_buf, z_buf, acc, s_plane, s_line,
    h_lam, h_back, h_a, h_slope, h_g2,
    small_sem, out_sem, in_sem, ring_send, ring_recv, z_send, z_recv, s_send, s_recv,
):
    g = lax.axis_index("grp")
    path = lax.axis_index("path")
    x, z = path // Z, lax.rem(path, Z)

    def owner(pair, k):
        owner_x, hops = place(pair, k, x)
        return owner_x, lax.rem(z + hops, Z)

    def fetches(pair):
        return [
            pltpu.make_async_copy(hbm.at[owner(pair, k)], vmem.at[pair, k], in_sem.at[i, pair // 4])
            for k in range(2)
            for i, (hbm, vmem) in enumerate(((load_hbm, load_v), (z_hbm, z_v), (cot_hbm, cot_v)))
        ]

    small = [
        pltpu.make_async_copy(hbm, here, small_sem.at[i])
        for i, (hbm, here) in enumerate(((stress_hbm, stress_ref), (first_hbm, first_ref), (start_hbm, start_ref)))
    ]
    for copy in small:
        copy.start()

    @pl.loop(0, 4)
    def _(pair):
        for copy in fetches(pair):
            copy.start()

    def x_peer(k):
        return (g, lax.rem(x + k, X) * Z + z)

    def z_peer(k):
        return (g, x * Z + lax.rem(z + k, Z))

    y, core = g // CORES, lax.rem(g, CORES)

    def plane_peer(k):
        return (lax.rem(y + k // X, Y) * CORES + core, lax.rem(x + k % X, X) * Z + z)

    def line_peer(k):
        return (y * CORES + lax.rem(core + k // Z, CORES), x * Z + lax.rem(z + k % Z, Z))

    barrier = pltpu.get_barrier_semaphore()
    for k in range(1, SIXTEEN):
        for peer in (plane_peer, line_peer):
            pl.semaphore_signal(barrier, inc=1, device_id=peer(k), device_id_type=MESH)

    @pl.loop(4, PAIRS)
    def _(pair):
        for copy in fetches(pair):
            copy.start()

    for copy in small:
        copy.wait()
    rows, cols = index_masks()
    eye = rows == cols
    stress_col = jnp.sum(jnp.where(eye, stress_ref[...], 0.0), axis=1, keepdims=True)
    acc[...] = jnp.zeros_like(acc)

    def ring(way, half, step):
        return pltpu.make_async_remote_copy(
            src_ref=out_buf.at[2 * STEPS[half, step] + way],
            dst_ref=ring_buf.at[half, step, way],
            send_sem=ring_send,
            recv_sem=ring_recv.at[half, step],
            device_id=x_peer(X - 1 if way else 1),
            device_id_type=MESH,
        )

    def hand_over(half, side, k):
        hops = 3 - 2 * half - side if k else 4 + 2 * half + side
        return pltpu.make_async_remote_copy(
            src_ref=out_buf.at[2 * STEPS[half, 3] + 1 - side, k],
            dst_ref=z_buf.at[hops - 1],
            send_sem=z_send,
            recv_sem=z_recv,
            device_id=z_peer(hops),
            device_id_type=MESH,
        )

    handed = [(0, side, k) for side in range(2) for k in range(2)], [(1, 0, 0), (1, 0, 1), (1, 1, 0)]

    def arrived(half, step):
        wait_for(ring_buf.at[half, step], ring_recv.at[half, step])

    def finish(half):
        arrived(half, 2)
        for way in range(2):
            out_buf[2 * STEPS[half, 3] + 1 - way] += ring_buf[half, 2, way]
        for what in handed[half]:
            hand_over(*what).start()

    def emit(d, bar, total):
        pack(d["out"], bar, total)
        acc[...] += d["load"][...] * bar

    def scenario(pair, k):
        owner_x, owner_z = owner(pair, k)
        s = owner_x * Z + owner_z
        return dict(
            load=load_v.at[pair, k], z=z_v.at[pair, k], cot=cot_v.at[pair, k], out=out_buf.at[pair, k],
            first=first_ref[s], r0=start_ref[pl.ds(s, 1), :],
        )

    def share(buf, peer, me, stage):
        return [
            pltpu.make_async_remote_copy(
                src_ref=buf.at[me],
                dst_ref=buf.at[me],
                send_sem=s_send.at[stage],
                recv_sem=s_recv.at[stage],
                device_id=peer(k),
                device_id_type=MESH,
            )
            for k in range(1, SIXTEEN)
        ]

    stage_plane = share(s_plane, plane_peer, y * X + x, 0)
    stage_line = share(s_line, line_peer, core * Z + z, 1)

    masks = (jnp.where(rows >= cols, LN2, 0.0), jnp.where(rows <= cols, LN2 * LN2, 0.0))
    held = dict(lam=h_lam, back=h_back, a=h_a, slope=h_slope, g2=h_g2)

    def items(group):
        return [scenario(4 * group + j, k) for j in range(4) for k in range(2)]

    def start(group, slot):
        blocks = pl.ds(4 * group, 4)
        for i, vmem in enumerate((load_v, z_v, cot_v)):
            wait_for(vmem.at[blocks], in_sem.at[i, group])
        return forward(items(group), held, slot, masks, stress_col, log_paths)

    def send(half, step):
        for way in range(2):
            ring(way, half, step).start()

    def take(half, step):
        arrived(half, step - 2)
        for way in range(2):
            out_buf[2 * STEPS[half, step] + way] += ring_buf[half, step - 2, way]

    interleaved(start(0, 0))

    @pl.loop(1, 4)
    def _(group):
        slot = lax.rem(group, 2)
        ahead = start(group, slot)
        interleaved(adjoint(items(group - 1), held, 1 - slot, emit), ahead)

        @pl.when(group == 1)
        def _():
            pl.semaphore_wait(barrier, 2 * (SIXTEEN - 1))
            send(0, 0)
            send(0, 1)

        @pl.when(group == 2)
        def _():
            send(1, 0)

        @pl.when(group == 3)
        def _():
            take(0, 2)
            send(0, 2)

    interleaved(adjoint(items(3), held, 1, emit))
    part = jnp.sum(jnp.where(eye, jnp.sum(acc[...], axis=1, keepdims=True), 0.0), axis=0, keepdims=True)
    s_plane[y * X + x] = jnp.concatenate([part, jnp.zeros((1, 128 - NR), f32)], axis=1)
    for copy in stage_plane:
        copy.start()
    take(1, 2)
    send(1, 2)
    send(1, 1)
    take(0, 3)
    finish(0)

    wait_for(s_plane.at[pl.ds(0, SIXTEEN - 1)], s_recv.at[0])
    s_line[core * Z + z] = jnp.sum(s_plane[...], axis=0)
    for copy in stage_line:
        copy.start()

    take(1, 3)
    finish(1)

    lam = scaled_loadings(load_v[14, 1], stress_col, first_ref[path], rows)
    lh, ll = split(lam)
    cov = (dot_nt(lh, lh) + dot_nt(lh, ll) + dot_nt(ll, lh)) * (LN2 * LN2)
    r0 = start_ref[pl.ds(path, 1), :]

    wait_for(z_buf, z_recv)
    bar, total = unpack(out_buf[14, 1] + jnp.sum(z_buf[...], axis=0))
    out[0:NR, 0:NR] = stress_col * bar
    through = jnp.sum(jnp.where(rows >= cols, cov, 0.0) * total, axis=0, keepdims=True)
    direct = jnp.sum(jnp.where(eye, total, 0.0), axis=0, keepdims=True)
    out[80:81, 0:NR] = direct / r0 + through * (100.0 / ((100.0 + r0) * (100.0 + r0)))

    results = [
        pltpu.make_async_copy(out.at[part], out_hbm.at[part], out_sem.at[i])
        for i, part in enumerate((pl.ds(0, 88), pl.ds(88, 8)))
    ]
    results[0].start()

    wait_for(out_buf.at[pl.ds(0, 12)], ring_send)
    wait_for(z_buf, z_send)
    for stage in range(2):
        wait_for(s_line.at[pl.ds(0, SIXTEEN - 1)], s_send.at[stage])
    wait_for(s_line.at[pl.ds(0, SIXTEEN - 1)], s_recv.at[1])
    out[88:89] = jnp.sum(s_line[...], axis=0)
    results[1].start()

    for copy in results:
        copy.wait()


def hand_on(packed, rate_out, vol_out, stress_out):
    rate_out[...] = packed[80:81, 0:NR]
    vol_out[0] = packed[0:NR, 0:NR]
    stress_out[...] = packed[88:89, 0:NR]


def body(start_rates, loadings, stress, increments, cotangent, first_active):
    log_paths = math.log2(WIDTH * X * Z)
    vmem = pl.BlockSpec(memory_space=pltpu.VMEM)
    anywhere = pl.BlockSpec(memory_space=pl.ANY)
    dma = pltpu.SemaphoreType.DMA
    summed = pl.pallas_call(
        lambda *refs: kernel(log_paths, *refs),
        out_shape=jax.ShapeDtypeStruct((96, 128), f32),
        in_specs=[anywhere] * 6,
        out_specs=anywhere,
        scratch_shapes=[
            pltpu.VMEM((1, NR), f32),
            pltpu.SMEM((2 * PAIRS,), jnp.int32),
            pltpu.VMEM((2 * PAIRS, NR), f32),
            pltpu.VMEM((96, 128), f32),
            pltpu.VMEM((PAIRS, 2, NR, NR), f32),
            pltpu.VMEM((PAIRS, 2, 2, NR, WIDTH), bf16),
            pltpu.VMEM((PAIRS, 2, NR, WIDTH), f32),
            pltpu.VMEM((PAIRS, 2, PACKED, 128), f32),
            pltpu.VMEM((2, 3, 2, 2, PACKED, 128), f32),
            pltpu.VMEM((Z - 1, PACKED, 128), f32),
            pltpu.VMEM((NR, NR), f32),
            pltpu.VMEM((SIXTEEN, 1, 128), f32),
            pltpu.VMEM((SIXTEEN, 1, 128), f32),
            pltpu.VMEM((2, 8, NR, NR), f32),
            pltpu.VMEM((2, 8, NR, NR), bf16),
            pltpu.VMEM((2, 8, NR, WIDTH), bf16),
            pltpu.VMEM((2, 8, NR, WIDTH), f32),
            pltpu.VMEM((2, 8, NR, WIDTH), f32),
            dma((3,)),
            dma((2,)),
            dma((3, 4)),
            dma(()),
            dma((2, 3)),
            dma(()),
            dma(()),
            dma((2,)),
            dma((2,)),
        ],
        compiler_params=pltpu.CompilerParams(
            collective_id=0, has_side_effects=True, vmem_limit_bytes=56 * 2**20
        ),
        name="adjoint",
    )(
        stress[None],
        first_active,
        start_rates,
        loadings.reshape(X, Z, NR, NR),
        increments.reshape(X, Z, 2, NR, WIDTH),
        cotangent.reshape(X, Z, NR, WIDTH),
    )
    rate, vol, stress_gradient = pl.pallas_call(
        hand_on,
        out_shape=(
            jax.ShapeDtypeStruct((1, NR), f32),
            jax.ShapeDtypeStruct((1, NR, NR), f32),
            jax.ShapeDtypeStruct((1, NR), f32),
        ),
        in_specs=[vmem],
        out_specs=(vmem, vmem, vmem),
        name="results",
    )(summed)
    return rate, vol, stress_gradient[0]


def solution(mesh):
    return jax.shard_map(
        body,
        mesh=mesh,
        in_specs=(
            P("grp", None),
            P("grp", None, None),
            P(),
            P("grp", None, None, "path"),
            P("grp", None, "path"),
            P("grp"),
        ),
        out_specs=(P(("grp", "path"), None), P(("grp", "path"), None, None), P()),
        check_vma=False,
    )
```

```python
import math

import jax
import jax.numpy as jnp
from jax import lax
from jax.experimental import pallas as pl
from jax.experimental.pallas import tpu as pltpu
from jax.sharding import PartitionSpec as P

NR = 80
WIDTH = 256
X, Z = 4, 8
Y, CORES = 4, 2
SIXTEEN = X * Y
PAIRS = 16
PACKED = 56
LN2 = math.log(2.0)
LOG2E = 1.0 / LN2
bf16 = jnp.bfloat16
f32 = jnp.float32
MESH = pl.DeviceIdType.MESH


def dot(a, b):
    return jnp.dot(a, b, preferred_element_type=f32)


def dot_nt(a, b):
    return lax.dot_general(a, b, (((1,), (1,)), ((), ())), preferred_element_type=f32)


def split(value):
    high = value.astype(bf16)
    return high, (value - high.astype(f32)).astype(bf16)


def index_masks():
    rows = lax.broadcasted_iota(jnp.int32, (NR, NR), 0)
    cols = lax.broadcasted_iota(jnp.int32, (NR, NR), 1)
    return rows, cols


STEPS = {(0, 0): 0, (0, 1): 1, (1, 0): 2, (0, 2): 3, (1, 1): 4, (0, 3): 5, (1, 2): 6, (1, 3): 7}


def place(pair, k, x):
    at, way = pair // 2, pair % 2
    half = (at + 1) % 2 - (7 - at) // 7 + at // 7
    step = (at + 1 - 2 * half) // 2
    reach = 2 - (step + 1) // 2
    side = lax.rem(step + way, 2)
    hops = 3 - 2 * half - side if k else 4 + 2 * half + side
    return lax.rem(x + reach * (1 - way) + (X - reach) * way, X), hops


def scaled_loadings(load, stress_col, first, rows):
    return load * jnp.where(rows >= first, stress_col * LOG2E, 0.0)


def forward(items, held, slot, masks, stress_col, log_paths):
    rows, cols = index_masks()
    eye = rows == cols
    pad = jnp.zeros((NR, 128 - NR), bf16)
    gap = jnp.zeros((128 - NR, WIDTH), bf16)
    for k, d in enumerate(items):
        yield
        d["lam"] = scaled_loadings(d["load"][...], stress_col, d["first"], rows)
        d["lh"], d["ll"] = split(d["lam"])
        held["lam"][slot, k] = d["lam"]
    for d in items:
        yield
        d["cov"] = dot_nt(d["lh"], d["lh"])
    for k, d in enumerate(items):
        yield
        drift = d["cov"] * masks[0]
        r0 = d["r0"]
        accrual = r0 / (100.0 + r0)
        half = jnp.sum(d["lam"] * d["lam"], axis=1, keepdims=True) * (-0.5 * LN2)
        c1 = jnp.sum(drift * accrual + jnp.where(eye, jnp.log2(r0), 0.0), axis=1, keepdims=True)
        d["c1"] = half + c1 - math.log2(100.0)
        d["c2"] = half + (math.log2(100.0) - log_paths)
        d["left"] = jnp.concatenate([d["lh"], pad, d["ll"]], axis=1)
        d["drift"] = drift.astype(bf16)
        held["back"][slot, k] = (d["cov"] * masks[1]).astype(bf16)
    for d in items:
        yield
        z1 = d["z"][0]
        d["e1"] = dot(d["left"], jnp.concatenate([z1, gap, z1], axis=0))
    for k, d in enumerate(items):
        yield
        mid = jnp.exp2(d["e1"] + d["c1"])
        inverse = 1.0 / (1.0 + mid)
        accrual = mid * inverse
        d["mid"], d["a"] = mid, accrual.astype(bf16)
        held["a"][slot, k] = d["a"]
        held["slope"][slot, k] = accrual * inverse
    for d in items:
        yield
        z2 = d["z"][1]
        d["e2"] = dot(d["left"], jnp.concatenate([z2, gap, z2], axis=0)) + dot(d["drift"], d["a"])
    for k, d in enumerate(items):
        yield
        held["g2"][slot, k] = d["mid"] * jnp.exp2(d["e2"] + d["c2"]) * d["cot"][...]


def adjoint(items, held, slot, emit):
    rows, cols = index_masks()
    low = rows >= cols
    ones = jnp.ones((16, WIDTH), bf16)
    many = jnp.ones((128, WIDTH), bf16)
    gap = jnp.zeros((32, WIDTH), bf16)
    for k, d in enumerate(items):
        yield
        d["g2"] = held["g2"][slot, k]
        d["g2h"], d["g2l"] = split(d["g2"])
    for k, d in enumerate(items):
        yield
        d["da"] = dot(held["back"][slot, k], d["g2h"])
    for k, d in enumerate(items):
        yield
        right = jnp.concatenate([d["z"][1], ones, gap, held["a"][slot, k]], axis=0)
        d["sums2"] = dot_nt(jnp.concatenate([d["g2h"], d["g2l"]], axis=0), right)
    for k, d in enumerate(items):
        yield
        g1h, g1l = split(d["g2"] + held["slope"][slot, k] * d["da"])
        right = jnp.concatenate([d["z"][0], many], axis=0)
        d["sums1"] = dot_nt(jnp.concatenate([g1h, g1l], axis=0), right)
    for k, d in enumerate(items):
        yield
        lam = held["lam"][slot, k]
        lh, ll = split(lam)
        sum1 = d["sums1"][:NR, :128] + d["sums1"][NR:, :128]
        whole1 = d["sums1"][:NR, 128:208] + d["sums1"][NR:, 128:208]
        sum2 = d["sums2"][:NR, :128] + d["sums2"][NR:, :128]
        outer = d["sums2"][:NR, 128:208] + d["sums2"][NR:, 128:208]
        total2 = sum2[:, NR : NR + 1]
        bar_cov = jnp.where(low, outer + whole1 * (d["r0"] / (100.0 + d["r0"])), 0.0)
        mh, ml = split((bar_cov + bar_cov.T) * LN2)
        both = dot(jnp.concatenate([mh, ml], axis=0), lh)
        through = both[:NR] + both[NR:] + dot(mh, ll)
        bar = sum1[:, :NR] + sum2[:, :NR] + through - ((whole1 + total2) * LN2) * lam
        emit(d, jnp.where(rows >= d["first"], bar, 0.0), sum1)


def interleaved(*parts):
    parts = list(parts)
    while parts:
        for part in list(parts):
            if next(part, parts) is parts:
                parts.remove(part)


def wait_for(ref, sem):
    pltpu.make_async_copy(ref, ref, sem).wait()


def pack(ref, bar, spread):
    ref[:, 0:NR] = bar[:PACKED]
    ref[:, NR:128] = spread[:PACKED, NR:128]
    ref[0:24, 81:128] = bar[PACKED:, 0:47]
    ref[24:48, 81:114] = bar[PACKED:, 47:NR]
    ref[24:48, 114:115] = spread[PACKED:, 114:115]


def unpack(value):
    rest = jnp.concatenate([value[0:24, 81:128], value[24:48, 81:115]], axis=1)
    bar = jnp.concatenate([value[:, 0:NR], rest[:, 0:NR]], axis=0)
    total = jnp.concatenate([value[:, NR : NR + 1], rest[:, NR : NR + 1]], axis=0)
    return bar, total


def kernel(
    log_paths,
    stress_hbm, first_hbm, start_hbm, load_hbm, z_hbm, cot_hbm,
    out_hbm,
    stress_ref, first_ref, start_ref, out,
    load_v, z_v, cot_v, out_buf, ring_buf, z_buf, acc, s_plane, s_line,
    h_lam, h_back, h_a, h_slope, h_g2,
    small_sem, out_sem, in_sem, ring_send, ring_recv, z_send, z_recv, s_send, s_recv,
):
    g = lax.axis_index("grp")
    path = lax.axis_index("path")
    x, z = path // Z, lax.rem(path, Z)

    def owner(pair, k):
        owner_x, hops = place(pair, k, x)
        return owner_x, lax.rem(z + hops, Z)

    def fetches(pair):
        return [
            pltpu.make_async_copy(hbm.at[owner(pair, k)], vmem.at[pair, k], in_sem.at[i, pair // 4])
            for k in range(2)
            for i, (hbm, vmem) in enumerate(((load_hbm, load_v), (z_hbm, z_v), (cot_hbm, cot_v)))
        ]

    small = [
        pltpu.make_async_copy(hbm, here, small_sem.at[i])
        for i, (hbm, here) in enumerate(((stress_hbm, stress_ref), (first_hbm, first_ref), (start_hbm, start_ref)))
    ]
    for copy in small:
        copy.start()

    @pl.loop(0, 4)
    def _(pair):
        for copy in fetches(pair):
            copy.start()

    def x_peer(k):
        return (g, lax.rem(x + k, X) * Z + z)

    def z_peer(k):
        return (g, x * Z + lax.rem(z + k, Z))

    y, core = g // CORES, lax.rem(g, CORES)

    def plane_peer(k):
        return (lax.rem(y + k // X, Y) * CORES + core, lax.rem(x + k % X, X) * Z + z)

    def line_peer(k):
        return (y * CORES + lax.rem(core + k // Z, CORES), x * Z + lax.rem(z + k % Z, Z))

    barrier = pltpu.get_barrier_semaphore()
    for k in range(1, SIXTEEN):
        for peer in (plane_peer, line_peer):
            pl.semaphore_signal(barrier, inc=1, device_id=peer(k), device_id_type=MESH)

    @pl.loop(4, PAIRS)
    def _(pair):
        for copy in fetches(pair):
            copy.start()

    for copy in small:
        copy.wait()
    rows, cols = index_masks()
    eye = rows == cols
    stress_col = jnp.sum(jnp.where(eye, stress_ref[...], 0.0), axis=1, keepdims=True)
    acc[...] = jnp.zeros_like(acc)

    def ring(way, half, step):
        return pltpu.make_async_remote_copy(
            src_ref=out_buf.at[2 * STEPS[half, step] + way],
            dst_ref=ring_buf.at[half, step, way],
            send_sem=ring_send,
            recv_sem=ring_recv.at[half, step],
            device_id=x_peer(X - 1 if way else 1),
            device_id_type=MESH,
        )

    def hand_over(half, side, k):
        hops = 3 - 2 * half - side if k else 4 + 2 * half + side
        return pltpu.make_async_remote_copy(
            src_ref=out_buf.at[2 * STEPS[half, 3] + 1 - side, k],
            dst_ref=z_buf.at[hops - 1],
            send_sem=z_send,
            recv_sem=z_recv,
            device_id=z_peer(hops),
            device_id_type=MESH,
        )

    handed = [(0, side, k) for side in range(2) for k in range(2)], [(1, 0, 0), (1, 0, 1), (1, 1, 0)]

    def arrived(half, step):
        wait_for(ring_buf.at[half, step], ring_recv.at[half, step])

    def finish(half):
        arrived(half, 2)
        for way in range(2):
            out_buf[2 * STEPS[half, 3] + 1 - way] += ring_buf[half, 2, way]
        for what in handed[half]:
            hand_over(*what).start()

    def emit(d, bar, spread):
        pack(d["out"], bar, spread)
        acc[...] += d["load"][...] * bar

    def scenario(pair, k):
        owner_x, owner_z = owner(pair, k)
        s = owner_x * Z + owner_z
        return dict(
            load=load_v.at[pair, k], z=z_v.at[pair, k], cot=cot_v.at[pair, k], out=out_buf.at[pair, k],
            first=first_ref[s], r0=start_ref[pl.ds(s, 1), :],
        )

    def share(buf, peer, me, stage):
        return [
            pltpu.make_async_remote_copy(
                src_ref=buf.at[me],
                dst_ref=buf.at[me],
                send_sem=s_send.at[stage],
                recv_sem=s_recv.at[stage],
                device_id=peer(k),
                device_id_type=MESH,
            )
            for k in range(1, SIXTEEN)
        ]

    stage_plane = share(s_plane, plane_peer, y * X + x, 0)
    stage_line = share(s_line, line_peer, core * Z + z, 1)

    masks = (jnp.where(rows >= cols, LN2, 0.0), jnp.where(rows <= cols, LN2 * LN2, 0.0))
    held = dict(lam=h_lam, back=h_back, a=h_a, slope=h_slope, g2=h_g2)

    def items(group):
        return [scenario(4 * group + j, k) for j in range(4) for k in range(2)]

    def start(group, slot):
        blocks = pl.ds(4 * group, 4)
        for i, vmem in enumerate((load_v, z_v, cot_v)):
            wait_for(vmem.at[blocks], in_sem.at[i, group])
        return forward(items(group), held, slot, masks, stress_col, log_paths)

    def send(half, step):
        for way in range(2):
            ring(way, half, step).start()

    def take(half, step):
        arrived(half, step - 2)
        for way in range(2):
            out_buf[2 * STEPS[half, step] + way] += ring_buf[half, step - 2, way]

    interleaved(start(0, 0))

    @pl.loop(1, 4)
    def _(group):
        slot = lax.rem(group, 2)
        ahead = start(group, slot)
        interleaved(adjoint(items(group - 1), held, 1 - slot, emit), ahead)

        @pl.when(group == 1)
        def _():
            pl.semaphore_wait(barrier, 2 * (SIXTEEN - 1))
            send(0, 0)
            send(0, 1)

        @pl.when(group == 2)
        def _():
            send(1, 0)

        @pl.when(group == 3)
        def _():
            take(0, 2)
            send(0, 2)

    interleaved(adjoint(items(3), held, 1, emit))
    part = jnp.sum(jnp.where(eye, jnp.sum(acc[...], axis=1, keepdims=True), 0.0), axis=0, keepdims=True)
    s_plane[y * X + x] = jnp.concatenate([part, jnp.zeros((1, 128 - NR), f32)], axis=1)
    for copy in stage_plane:
        copy.start()
    take(1, 2)
    send(1, 2)
    send(1, 1)
    take(0, 3)
    finish(0)

    wait_for(s_plane.at[pl.ds(0, SIXTEEN - 1)], s_recv.at[0])
    s_line[core * Z + z] = jnp.sum(s_plane[...], axis=0)
    for copy in stage_line:
        copy.start()

    take(1, 3)
    finish(1)

    lam = scaled_loadings(load_v[14, 1], stress_col, first_ref[path], rows)
    lh, ll = split(lam)
    cov = (dot_nt(lh, lh) + dot_nt(lh, ll) + dot_nt(ll, lh)) * (LN2 * LN2)
    r0 = start_ref[pl.ds(path, 1), :]

    wait_for(z_buf, z_recv)
    bar, total = unpack(out_buf[14, 1] + jnp.sum(z_buf[...], axis=0))
    out[0:NR, 0:NR] = stress_col * bar
    through = jnp.sum(jnp.where(rows >= cols, cov, 0.0) * total, axis=0, keepdims=True)
    direct = jnp.sum(jnp.where(eye, total, 0.0), axis=0, keepdims=True)
    out[80:81, 0:NR] = direct / r0 + through * (100.0 / ((100.0 + r0) * (100.0 + r0)))

    results = [
        pltpu.make_async_copy(out.at[part], out_hbm.at[part], out_sem.at[i])
        for i, part in enumerate((pl.ds(0, 88), pl.ds(88, 8)))
    ]
    results[0].start()

    wait_for(out_buf.at[pl.ds(0, 12)], ring_send)
    wait_for(z_buf, z_send)
    for stage in range(2):
        wait_for(s_line.at[pl.ds(0, SIXTEEN - 1)], s_send.at[stage])
    wait_for(s_line.at[pl.ds(0, SIXTEEN - 1)], s_recv.at[1])
    out[88:89] = jnp.sum(s_line[...], axis=0)
    results[1].start()

    for copy in results:
        copy.wait()


def hand_on(packed, rate_out, vol_out, stress_out):
    rate_out[...] = packed[80:81, 0:NR]
    vol_out[0] = packed[0:NR, 0:NR]
    stress_out[...] = packed[88:89, 0:NR]


def body(start_rates, loadings, stress, increments, cotangent, first_active):
    log_paths = math.log2(WIDTH * X * Z)
    vmem = pl.BlockSpec(memory_space=pltpu.VMEM)
    anywhere = pl.BlockSpec(memory_space=pl.ANY)
    dma = pltpu.SemaphoreType.DMA
    summed = pl.pallas_call(
        lambda *refs: kernel(log_paths, *refs),
        out_shape=jax.ShapeDtypeStruct((96, 128), f32),
        in_specs=[anywhere] * 6,
        out_specs=anywhere,
        scratch_shapes=[
            pltpu.VMEM((1, NR), f32),
            pltpu.SMEM((2 * PAIRS,), jnp.int32),
            pltpu.VMEM((2 * PAIRS, NR), f32),
            pltpu.VMEM((96, 128), f32),
            pltpu.VMEM((PAIRS, 2, NR, NR), f32),
            pltpu.VMEM((PAIRS, 2, 2, NR, WIDTH), bf16),
            pltpu.VMEM((PAIRS, 2, NR, WIDTH), f32),
            pltpu.VMEM((PAIRS, 2, PACKED, 128), f32),
            pltpu.VMEM((2, 3, 2, 2, PACKED, 128), f32),
            pltpu.VMEM((Z - 1, PACKED, 128), f32),
            pltpu.VMEM((NR, NR), f32),
            pltpu.VMEM((SIXTEEN, 1, 128), f32),
            pltpu.VMEM((SIXTEEN, 1, 128), f32),
            pltpu.VMEM((2, 8, NR, NR), f32),
            pltpu.VMEM((2, 8, NR, NR), bf16),
            pltpu.VMEM((2, 8, NR, WIDTH), bf16),
            pltpu.VMEM((2, 8, NR, WIDTH), f32),
            pltpu.VMEM((2, 8, NR, WIDTH), f32),
            dma((3,)),
            dma((2,)),
            dma((3, 4)),
            dma(()),
            dma((2, 3)),
            dma(()),
            dma(()),
            dma((2,)),
            dma((2,)),
        ],
        compiler_params=pltpu.CompilerParams(
            collective_id=0, has_side_effects=True, vmem_limit_bytes=56 * 2**20
        ),
        name="adjoint",
    )(
        stress[None],
        first_active,
        start_rates,
        loadings.reshape(X, Z, NR, NR),
        increments.reshape(X, Z, 2, NR, WIDTH),
        cotangent.reshape(X, Z, NR, WIDTH),
    )
    rate, vol, stress_gradient = pl.pallas_call(
        hand_on,
        out_shape=(
            jax.ShapeDtypeStruct((1, NR), f32),
            jax.ShapeDtypeStruct((1, NR, NR), f32),
            jax.ShapeDtypeStruct((1, NR), f32),
        ),
        in_specs=[vmem],
        out_specs=(vmem, vmem, vmem),
        name="results",
    )(summed)
    return rate, vol, stress_gradient[0]


def solution(mesh):
    return jax.shard_map(
        body,
        mesh=mesh,
        in_specs=(
            P("grp", None),
            P("grp", None, None),
            P(),
            P("grp", None, None, "path"),
            P("grp", None, "path"),
            P("grp"),
        ),
        out_specs=(P(("grp", "path"), None), P(("grp", "path"), None, None), P()),
        check_vma=False,
    )
```
